128 devices in a mesh: chain: 8 (over x, z_lo), dp: 16 (over z_hi, y, core).
Axes of the slice: x: 4, y: 4, z: 4 (z_hi: 2, z_lo: 2; z = z_hi * 2 + z_lo), core: 2. Of those that a mesh axis runs over, the one named last changes fastest.
Arguments:
- tokens: bfloat16 [4, 1024, 3072], P(None, 'dp'), may hold values from -6 to 6
- cotangent: bfloat16 [4, 1024, 3072], P(None, 'dp'), may hold values from -6 to 6
- weights: bfloat16 [8, 3072, 3072], P('chain'), may hold values from -0.109375 to 0.109375
- gains: float32 [8, 3072], P('chain'), may hold values from 0.1 to 1.9
Outputs:
- weight_grad: bfloat16 [8, 3072, 3072], P('chain', 'dp')
- gain_grad: float32 [8, 3072], P('chain', 'dp')
The draws below stay inside these ranges and needn't reach their ends.
All inputs are finite; a program needn't handle non-finite values.
Results may differ from the reference program's by a relative error of at most 0.029.
Values may be sent and summed in bfloat16 or wider, within the bound.
No kernel may reach another device: no remote copies, remote signals or barrier semaphores. Data moves between devices by JAX's collectives and lax.ppermute only.
A program may use at most 192 MiB of HBM per device.

```python
import jax
import jax.numpy as jnp
from jax import lax

D = 3072
MB = 4
MBR = 64
SECTIONS = 8
TOK = 1024
N_CHAIN = 8
N_DP = 16


def raised(result, key, source, target, blocks, factor):
    def block_of(dim):
        return (jnp.arange(result.shape[dim]) // (result.shape[dim] // blocks)).reshape((-1,) + (1,) * (result.ndim - 1 - dim))

    first = jax.random.permutation(key, blocks)[block_of(target)]
    second = (block_of(target) + blocks // 2) % blocks
    return jnp.where((block_of(source) == first) | (block_of(source) == second), factor * result, result)


def levels(rng, shape, shards, smallest, top_value):
    level, own = 1.0, jax.random.fold_in(rng, 6)
    for position, shards_of in shards:
        steps = jnp.exp(jax.random.uniform(jax.random.fold_in(own, position), (shards_of,), jnp.float32, smallest / len(shards), top_value / len(shards)))
        level = level * jnp.repeat(steps, shape[position] // shards_of).reshape([-1 if axis == position else 1 for axis in range(len(shape))])
    return level


def gaussian(rng, extent, spread, bound, split=(), held_as=jnp.bfloat16):
    factor_of = levels(rng, extent, split, -0.22, 0.18) if split else 1.0
    values = jax.random.normal(rng, extent, jnp.float32) * spread * factor_of
    return jnp.minimum(jnp.maximum(values, -bound), bound).astype(held_as)


def noise_with(own_key, extent, deviation, limit, cuts, heavy, dtype=jnp.bfloat16):
    drawn = deviation * jax.random.normal(own_key, extent, jnp.float32)
    if cuts:
        drawn = drawn * levels(own_key, extent, cuts, -0.22, 0.18)
    return jnp.clip(raised(drawn, jax.random.fold_in(own_key, 3), *heavy), -limit, limit).astype(dtype)


def setup_inputs(seed: int = 0) -> dict:
    streams_of = jax.random.split(jax.random.key(seed), 5)
    tokens = noise_with(streams_of[0], (MB, TOK, D), 1.0, 6.0, ((1, 16),), (1, 2, 16, 2.0))
    cotangent = gaussian(streams_of[1], (MB, TOK, D), 1.0, 6.0, ((1, 16),))
    weights = gaussian(streams_of[2], (SECTIONS, D, D), D ** -0.5, 0.109375, ((0, 8),))
    gains = jnp.clip(1.0 + 0.18 * jax.random.normal(streams_of[3], (SECTIONS, D), jnp.float32), 0.1, 1.9)
    return dict(tokens=tokens, cotangent=cotangent, weights=weights, gains=gains)


def layer_parts(block_input, gain_row, weight):
    x_float = block_input.astype(jnp.float32)
    inv_rms = lax.rsqrt(lax.optimization_barrier(jnp.mean(x_float * x_float, axis=-1, keepdims=True)) + 1e-06)
    normed = x_float * inv_rms
    scaled = (normed * gain_row).astype(jnp.bfloat16)
    hidden = jnp.dot(scaled, weight, preferred_element_type=jnp.float32)
    return (x_float, inv_rms, normed, scaled, hidden)

def replica_rows(array):
    return array.reshape(MB, N_DP, MBR, D).transpose(1, 0, 2, 3).reshape(N_DP * MB * MBR, D)

def reference(tokens, cotangent, weights, gains):
    span = MB * MBR
    current = replica_rows(tokens)
    saved = []
    for section_index in range(N_CHAIN):
        saved.append(current)
        x_float, inv_rms, normed, scaled, hidden = layer_parts(current, gains[section_index], weights[section_index])
        current = (x_float + jax.nn.gelu(hidden)).astype(jnp.bfloat16)
    upstream = replica_rows(cotangent)
    weight_list = [None] * N_CHAIN
    gain_list = [None] * N_CHAIN
    for section_index in range(N_CHAIN - 1, -1, -1):
        weight = weights[section_index]
        gain_row = gains[section_index]
        x_float, inv_rms, normed, scaled, hidden = layer_parts(saved[section_index], gain_row, weight)
        grad_in = upstream.astype(jnp.float32)
        _, pullback = jax.vjp(jax.nn.gelu, hidden)
        grad_hidden = pullback(grad_in)[0].astype(jnp.bfloat16)
        grad_scaled = lax.dot_general(grad_hidden, weight, (((1,), (1,)), ((), ())), preferred_element_type=jnp.float32)
        gain_terms = lax.optimization_barrier(jnp.sum((grad_scaled * normed).reshape(N_DP, span, D), axis=1))
        gain_terms = lax.optimization_barrier(gain_terms.astype(jnp.bfloat16)).astype(jnp.float32)
        gain_list[section_index] = lax.optimization_barrier(jnp.sum(gain_terms, axis=0))

        def add_replica(running, operands):
            term = lax.dot_general(operands[0], operands[1], (((0,), (0,)), ((), ())), preferred_element_type=jnp.float32)
            term = lax.optimization_barrier(term.astype(jnp.bfloat16)).astype(jnp.float32)
            return (running + term, None)
        summed, _ = lax.scan(add_replica, jnp.zeros((D, D), jnp.float32), (scaled.reshape(N_DP, span, D), grad_hidden.reshape(N_DP, span, D)))
        weight_list[section_index] = summed.astype(jnp.bfloat16)
        grad_normed = grad_scaled * gain_row
        grad_input = grad_in + inv_rms * (grad_normed - normed * lax.optimization_barrier(jnp.mean(grad_normed * normed, axis=-1, keepdims=True)))
        upstream = grad_input.astype(jnp.bfloat16)
    return (jnp.stack(weight_list), jnp.stack(gain_list))
```

```python
import functools

import jax
import jax.numpy as jnp
from jax import lax
from jax.experimental import pallas as pl
from jax.experimental.pallas import tpu as pltpu
from jax.sharding import PartitionSpec as P

SECTIONS = 8
MB = 4
LAST = SECTIONS - 1
TURN = 2 * LAST
VM = pl.BlockSpec(memory_space=pltpu.VMEM)
SM = pl.BlockSpec(memory_space=pltpu.SMEM)
COLS = 1024
PIECES = 6


def pin(array):
    return pltpu.with_memory_space_constraint(array, pltpu.VMEM)


def params(mib):
    return pltpu.CompilerParams(vmem_limit_bytes=mib << 20)


def partner(section, replica):
    z_hi, rest = divmod(replica, 8)
    core = rest % 2
    if section % 2 == 0 and core == 1:
        z_hi = 1 - z_hi
    return z_hi * 8 + rest


def route(sections, forward, replicas):
    pairs = []
    for section in sections:
        low = section if forward else section - 1
        for replica in range(replicas):
            here, there = low * replicas + replica, (low + 1) * replicas + partner(low, replica)
            pairs.append((here, there) if forward else (there, here))
    return pairs


def load_kernel(weight_hbm, weight_ref, turned_ref, hidden_ref, input_ref, scaled_ref, grad_ref, sem):
    copy = pltpu.make_async_copy(weight_hbm, weight_ref, sem)
    copy.start()
    copy.wait()


def load(weight, micro, rows, channels):
    kept = (micro, rows, channels)
    return pl.pallas_call(
        load_kernel,
        out_shape=[
            pltpu.VMEM((channels, channels), jnp.bfloat16),
            pltpu.VMEM((channels, channels), jnp.bfloat16),
            pltpu.VMEM(kept, jnp.float32),
            pltpu.VMEM(kept, jnp.bfloat16),
            pltpu.VMEM(kept, jnp.bfloat16),
            pltpu.VMEM(kept, jnp.bfloat16),
        ],
        in_specs=[pl.BlockSpec(memory_space=pl.ANY)],
        out_specs=[VM] * 6,
        scratch_shapes=[pltpu.SemaphoreType.DMA],
        name="load_weight",
        compiler_params=params(4),
    )(weight)


def turn_kernel(piece, weight_ref, turned_in, after_ref, turned_ref, token_ref):
    rows = weight_ref.shape[0] // PIECES
    step = 256
    for start in range(piece * rows, (piece + 1) * rows, step):
        turned_ref[:, start : start + step] = weight_ref[start : start + step, :].T
    token_ref[0] = 0


def turn(piece, weight, turned, after):
    return pl.pallas_call(
        functools.partial(turn_kernel, piece),
        out_shape=[
            jax.ShapeDtypeStruct(turned.shape, turned.dtype),
            jax.ShapeDtypeStruct((1,), jnp.int32),
        ],
        in_specs=[VM, VM, VM],
        out_specs=[VM, SM],
        input_output_aliases={1: 0},
        name="turn_weight",
        compiler_params=params(4),
    )(pin(weight), pin(turned), pin(after))


def forward_kernel(
    moment, section_ref, token_ref, given_ref, first_ref, gain_ref, weight_ref, _h, _i, _s,
    output_ref, hidden_ref, input_ref, scaled_ref,
):
    section = section_ref[0]
    slot = moment - section
    micro = hidden_ref.shape[0]

    @pl.when(jnp.logical_and(slot >= 0, slot < micro))
    def _():
        given = given_ref[...]
        if moment < micro:
            given = jnp.where(section == 0, first_ref[moment], given)
        input_ref[slot] = given
        x_float = given.astype(jnp.float32)
        inv_rms = lax.rsqrt(jnp.mean(x_float * x_float, axis=-1, keepdims=True) + 1e-06)
        scaled_ref[slot] = (x_float * inv_rms * gain_ref[...]).astype(jnp.bfloat16)
        for start in range(0, x_float.shape[1], COLS):
            part = slice(start, start + COLS)
            hidden = jnp.dot(scaled_ref[slot], weight_ref[:, part], preferred_element_type=jnp.float32)
            hidden_ref[slot, :, part] = hidden
            x_part = input_ref[slot, :, part].astype(jnp.float32)
            output_ref[:, part] = (x_part + jax.nn.gelu(hidden)).astype(jnp.bfloat16)


def forward(moment, section, token, given, first, gain, weight, kept):
    rows = jax.ShapeDtypeStruct(given.shape, given.dtype)
    hidden, inputs, scaled = kept
    return pl.pallas_call(
        functools.partial(forward_kernel, moment),
        out_shape=[pltpu.VMEM(rows.shape, rows.dtype)]
        + [jax.ShapeDtypeStruct(a.shape, a.dtype) for a in kept],
        in_specs=[SM, SM, VM, VM, VM, VM, VM, VM, VM],
        out_specs=[VM] * 4,
        input_output_aliases={6: 1, 7: 2, 8: 3},
        name=f"forward_step_{moment}",
        compiler_params=params(8),
    )(section, token, pin(given), pin(first), pin(gain), pin(weight), pin(hidden), pin(inputs), pin(scaled))


def backward_kernel(
    moment, section_ref, given_ref, last_ref, gain_ref, turned_ref, hidden_ref, input_ref, _g,
    output_ref, grad_ref, sum_ref,
):
    section = section_ref[0]
    slot = moment - TURN + section
    micro, rows, channels = hidden_ref.shape

    def upstream(part):
        given = given_ref[:, part]
        if 0 <= moment - LAST < micro:
            given = jnp.where(section == LAST, last_ref[moment - LAST, :, part], given)
        return given.astype(jnp.float32)

    active = jnp.logical_and(slot >= 0, slot < micro)

    @pl.when(active)
    def _():
        for start in range(0, channels, COLS):
            part = slice(start, start + COLS)
            _, pullback = jax.vjp(jax.nn.gelu, hidden_ref[slot, :, part])
            grad_ref[slot, :, part] = pullback(upstream(part))[0].astype(jnp.bfloat16)

    @pl.when(jnp.logical_and(active, section > 0))
    def _():
        x_float = input_ref[slot].astype(jnp.float32)
        inv_rms = lax.rsqrt(jnp.mean(x_float * x_float, axis=-1, keepdims=True) + 1e-06)
        total = jnp.zeros((rows, 1), jnp.float32)
        for start in range(0, channels, COLS):
            part = slice(start, start + COLS)
            grad_normed = gain_ref[:, part] * jnp.dot(
                grad_ref[slot], turned_ref[:, part], preferred_element_type=jnp.float32
            )
            sum_ref[:, part] = grad_normed
            normed = input_ref[slot, :, part].astype(jnp.float32) * inv_rms
            total = total + jnp.sum(grad_normed * normed, axis=-1, keepdims=True)
        mean = total * (1.0 / channels)
        for start in range(0, channels, COLS):
            part = slice(start, start + COLS)
            normed = input_ref[slot, :, part].astype(jnp.float32) * inv_rms
            grad_input = upstream(part) + inv_rms * (sum_ref[:, part] - normed * mean)
            output_ref[:, part] = grad_input.astype(jnp.bfloat16)


def backward(moment, section, given, last, gain, turned, hidden, inputs, grads):
    return pl.pallas_call(
        functools.partial(backward_kernel, moment),
        out_shape=[
            pltpu.VMEM(given.shape, given.dtype),
            jax.ShapeDtypeStruct(grads.shape, grads.dtype),
        ],
        in_specs=[SM, VM, VM, VM, VM, VM, VM, VM],
        out_specs=[VM] * 2,
        input_output_aliases={7: 1},
        scratch_shapes=[pltpu.VMEM(given.shape, jnp.float32)],
        name=f"backward_step_{moment}",
        compiler_params=params(8),
    )(section, pin(given), pin(last), pin(gain), pin(turned), pin(hidden), pin(inputs), pin(grads))


def on_device(tokens, cotangent, weights, gains):
    replicas = lax.axis_size("dp")
    micro, rows, channels = tokens.shape
    section = lax.axis_index("chain").astype(jnp.int32).reshape(1)
    gain = gains
    axes = ("chain", "dp")

    weight, turned, hidden, inputs, scaled, grads = load(weights[0], micro, rows, channels)
    token = jnp.zeros((1,), jnp.int32)
    arriving = tokens[0]
    returning = cotangent[0]
    for moment in range(TURN + micro):
        sent = None
        if moment < LAST + micro:
            output, hidden, inputs, scaled = forward(
                moment, section, token, arriving, tokens, gain, weight, (hidden, inputs, scaled)
            )
            senders = [s for s in range(LAST) if 0 <= moment - s < micro]
            if senders:
                sent = lax.ppermute(output, axes, route(senders, True, replicas))
            if moment < PIECES:
                turned, token = turn(moment, weight, turned, output)
        if moment >= LAST:
            output, grads = backward(
                moment, section, returning, cotangent, gain, turned, hidden, inputs, grads
            )
            senders = [s for s in range(1, SECTIONS) if 0 <= moment - TURN + s < micro]
            if senders:
                returning = lax.ppermute(output, axes, route(senders, False, replicas))
        if sent is not None:
            arriving = sent

    span = micro * rows
    every_scaled = lax.all_gather(scaled.reshape(span, channels), "dp", axis=0, tiled=True)
    share = channels // replicas
    columns = grads.reshape(span, replicas, share).transpose(1, 0, 2)
    columns = lax.all_to_all(columns, "dp", 0, 0).reshape(replicas * span, share)
    product = lax.dot_general(
        every_scaled, columns, (((0,), (0,)), ((), ())), preferred_element_type=jnp.float32
    ).astype(jnp.bfloat16)
    blocks = lax.all_to_all(product.reshape(replicas, share, share), "dp", 0, 0)
    weight_rows = blocks.transpose(1, 0, 2).reshape(share, channels)
    start = lax.axis_index("dp") * share
    own = lax.dynamic_slice_in_dim(weights[0], start, share, 0).astype(jnp.float32)
    own_gain = lax.dynamic_slice_in_dim(gains[0], start, share, 0)
    gain_rows = jnp.sum(own * weight_rows.astype(jnp.float32), axis=-1) / own_gain
    return (weight_rows[None], gain_rows[None])


def solution(mesh):
    placed = (P(None, "dp", None), P(None, "dp", None), P("chain", None, None), P("chain", None))
    return jax.shard_map(
        on_device,
        mesh=mesh,
        in_specs=placed,
        out_specs=(P("chain", "dp", None), P("chain", "dp")),
        check_vma=False,
    )
```

```python
import functools

import jax
import jax.numpy as jnp
from jax import lax
from jax.experimental import pallas as pl
from jax.experimental.pallas import tpu as pltpu
from jax.sharding import PartitionSpec as P

SECTIONS = 8
LAST = SECTIONS - 1
TURN = 2 * LAST
REPLICAS = 16
D = 3072
SPAN = 256
SHARE = D // REPLICAS
CHIPS = REPLICAS // 2
WIDE = D // CHIPS
STREAMS = 2
SLOTS = 2
ROWS = SPAN // (STREAMS * SLOTS)
COLS = 1024
PIECES = 6
PIECE = D // PIECES
TURNED = D
INPUT = 2 * D
GRAD = INPUT + SPAN
ENDS = GRAD + SPAN
HIGH = ENDS + SPAN
LOW = HIGH + SPAN
ARENA = LOW + SPAN
COST = pl.CostEstimate(flops=2 * ROWS * D * D, bytes_accessed=4 * D * D, transcendentals=0)
VM = pl.BlockSpec(memory_space=pltpu.VMEM)
ANY = pl.BlockSpec(memory_space=pl.ANY)


def pin(array):
    return pltpu.with_memory_space_constraint(array, pltpu.VMEM)


def far(array):
    return pltpu.with_memory_space_constraint(array, pltpu.HBM)


def params(mib):
    return pltpu.CompilerParams(vmem_limit_bytes=mib << 20)


def partner(section, replica):
    z_hi, rest = divmod(replica, 8)
    core = rest % 2
    if section % 2 == 0 and core == 1:
        z_hi = 1 - z_hi
    return z_hi * 8 + rest


def route(sections, forward):
    pairs = []
    for section in sections:
        low = section if forward else section - 1
        for replica in range(REPLICAS):
            here, there = low * REPLICAS + replica, (low + 1) * REPLICAS + partner(low, replica)
            pairs.append((here, there) if forward else (there, here))
    return pairs


def inverse_rms(x_float):
    return lax.rsqrt(jnp.mean(x_float * x_float, axis=-1, keepdims=True) + 1e-06)


def at_slot(base, slot):
    return pl.ds(pl.multiple_of(base + slot * ROWS, ROWS), ROWS)


def forward_block(slot, given, gain, arena, saved, output, scaled, sem, ready=None):
    arena[at_slot(INPUT, slot)] = given
    x_float = given.astype(jnp.float32)
    scaled[...] = (x_float * inverse_rms(x_float) * gain[...]).astype(jnp.bfloat16)
    save = pltpu.make_async_copy(scaled, saved.at[at_slot(0, slot)], sem)
    save.start()
    for index, start in enumerate(range(0, D, COLS)):
        part = slice(start, start + COLS)
        if ready is not None:
            ready(index)
        hidden = jnp.dot(scaled[...], arena[0:D, part], preferred_element_type=jnp.float32)
        high = hidden.astype(jnp.bfloat16)
        arena[at_slot(HIGH, slot), part] = high
        arena[at_slot(LOW, slot), part] = (hidden - high.astype(jnp.float32)).astype(jnp.bfloat16)
        x_part = arena[at_slot(INPUT, slot), part].astype(jnp.float32)
        output[:, part] = (x_part + jax.nn.gelu(hidden)).astype(jnp.bfloat16)
    save.wait()


def first_kernel(weight, tokens, cotangent, gain, output, arena, saved, scaled, sems):
    section = lax.axis_index("chain")
    ends = arena.at[pl.ds(ENDS, SPAN)]
    load_tokens = pltpu.make_async_copy(tokens, ends, sems.at[1])
    load_cotangent = pltpu.make_async_copy(cotangent, ends, sems.at[1])
    parts = [
        pltpu.make_async_copy(
            weight.at[:, pl.ds(start, COLS)], arena.at[pl.ds(0, D), pl.ds(start, COLS)], sems.at[2 + index]
        )
        for index, start in enumerate(range(0, D, COLS))
    ]
    @pl.when(section == 0)
    def _():
        load_tokens.start()

    for part in parts:
        part.start()

    @pl.when(section == LAST)
    def _():
        load_cotangent.start()

    @pl.when(section == 0)
    def _():
        load_tokens.wait()
        given = arena[ENDS : ENDS + ROWS]
        forward_block(
            0, given, gain, arena, saved, output, scaled, sems.at[0], lambda index: parts[index].wait()
        )

    @pl.when(section != 0)
    def _():
        for part in parts:
            part.wait()

    @pl.when(section == LAST)
    def _():
        load_cotangent.wait()


def first(weight, tokens, cotangent, gain):
    return pl.pallas_call(
        first_kernel,
        out_shape=[
            jax.ShapeDtypeStruct((ROWS, D), jnp.bfloat16),
            pltpu.VMEM((ARENA, D), jnp.bfloat16),
            jax.ShapeDtypeStruct((SPAN, D), jnp.bfloat16),
        ],
        in_specs=[ANY] * 3 + [VM],
        out_specs=[VM, VM, ANY],
        scratch_shapes=[pltpu.VMEM((ROWS, D), jnp.bfloat16), pltpu.SemaphoreType.DMA((2 + D // COLS,))],
        name="load_and_first_block",
        cost_estimate=COST,
        compiler_params=params(12),
    )(far(weight), far(tokens), far(cotangent), gain)


def turn_piece(piece, arena):
    step = 256
    for offset in range(0, PIECE, step):
        start = pl.multiple_of(piece * PIECE + offset, step)
        arena[TURNED : TURNED + D, pl.ds(start, step)] = arena[pl.ds(start, step), :].T


def forward_kernel(moment, stream, *refs):
    given_ref = refs[0] if moment else None
    gain, _, _, output, arena, saved, scaled, sem = refs[-8:]
    section = lax.axis_index("chain")
    place = moment - section
    active = jnp.logical_and(place >= 0, place < SLOTS)

    @pl.when(active)
    def _():
        start = ENDS + (stream * SLOTS + moment) * ROWS
        if moment == 0:
            given = arena[start : start + ROWS]
        elif moment < SLOTS:
            given = jnp.where(section == 0, arena[start : start + ROWS], given_ref[...])
        else:
            given = given_ref[...]
        forward_block(stream * SLOTS + place, given, gain, arena, saved, output, scaled, sem)

    if stream == STREAMS - 1 and moment < PIECES + SLOTS:
        piece = jnp.where(place < 0, moment, moment - SLOTS)

        @pl.when(jnp.logical_and(jnp.logical_not(active), piece < PIECES))
        def _():
            turn_piece(piece, arena)


def forward(moment, stream, given, gain, arena, saved):
    given = [given] if moment else []
    return pl.pallas_call(
        functools.partial(forward_kernel, moment, stream),
        out_shape=[
            jax.ShapeDtypeStruct((ROWS, D), jnp.bfloat16),
            jax.ShapeDtypeStruct(arena.shape, arena.dtype),
            jax.ShapeDtypeStruct(saved.shape, saved.dtype),
        ],
        in_specs=[VM] * (2 + len(given)) + [ANY],
        out_specs=[VM, VM, ANY],
        input_output_aliases={1 + len(given): 1, 2 + len(given): 2},
        scratch_shapes=[pltpu.VMEM((ROWS, D), jnp.bfloat16), pltpu.SemaphoreType.DMA],
        name=f"forward_{moment}_{stream}",
        cost_estimate=COST,
        compiler_params=params(6),
    )(*given, gain, pin(arena), saved)


def backward_kernel(moment, stream, held, pack, *refs):
    given_ref = refs[0] if moment > LAST else None
    gain = refs[0 if moment == LAST else 1]
    output, arena = refs[len(refs) - held - pack - 2 : len(refs) - held - pack]
    section = lax.axis_index("chain")
    place = moment - TURN + section
    slot = stream * SLOTS + place

    def upstream(part):
        start = ENDS + (stream * SLOTS + moment - LAST) * ROWS
        if moment == LAST:
            given = arena[start : start + ROWS, part]
        elif moment - LAST < SLOTS:
            given = jnp.where(section == LAST, arena[start : start + ROWS, part], given_ref[:, part])
        else:
            given = given_ref[:, part]
        return given.astype(jnp.float32)

    @pl.when(jnp.logical_and(place >= 0, place < SLOTS))
    def _():
        total = jnp.zeros((ROWS, 1), jnp.float32)
        for start in range(0, D, COLS):
            part = slice(start, start + COLS)
            high = arena[at_slot(HIGH, slot), part].astype(jnp.float32)
            hidden = high + arena[at_slot(LOW, slot), part].astype(jnp.float32)
            _, pullback = jax.vjp(jax.nn.gelu, hidden)
            grad_hidden = pullback(upstream(part))[0].astype(jnp.bfloat16)
            arena[at_slot(GRAD, slot), part] = grad_hidden
            total = total + jnp.sum(grad_hidden.astype(jnp.float32) * hidden, axis=-1, keepdims=True)

        @pl.when(section > 0)
        def _():
            inv_rms = inverse_rms(arena[at_slot(INPUT, slot)].astype(jnp.float32))
            mean = total * (1.0 / D)
            for start in range(0, D, COLS):
                part = slice(start, start + COLS)
                grad_normed = gain[:, part] * jnp.dot(
                    arena[at_slot(GRAD, slot)],
                    arena[TURNED : TURNED + D, part],
                    preferred_element_type=jnp.float32,
                )
                normed = arena[at_slot(INPUT, slot), part].astype(jnp.float32) * inv_rms
                grad_input = upstream(part) + inv_rms * (grad_normed - normed * mean)
                output[:, part] = grad_input.astype(jnp.bfloat16)

    if pack:
        packed = refs[-1]
        for chip in range(CHIPS):
            packed[chip] = arena[GRAD : GRAD + SPAN, chip * WIDE : (chip + 1) * WIDE].T


def backward(moment, stream, given, gain, arena, held, pack):
    given = [given] if moment > LAST else []
    count = len(given)
    return pl.pallas_call(
        functools.partial(backward_kernel, moment, stream, len(held), int(pack)),
        out_shape=[
            jax.ShapeDtypeStruct((ROWS, D), jnp.bfloat16),
            jax.ShapeDtypeStruct(arena.shape, arena.dtype),
        ]
        + [jax.ShapeDtypeStruct(a.shape, a.dtype) for a in held]
        + [jax.ShapeDtypeStruct((CHIPS, WIDE, SPAN), jnp.bfloat16)] * pack,
        in_specs=[VM] * (2 + count) + [ANY] * len(held),
        out_specs=[VM, VM] + [ANY] * len(held) + [VM] * pack,
        input_output_aliases={1 + count + i: 1 + i for i in range(1 + len(held))},
        name=f"backward_{moment}_{stream}",
        cost_estimate=COST,
        compiler_params=params(6),
    )(*given, gain, pin(arena), *held)


def product_kernel(grads, *refs):
    pieces, (keep, give, held, total, sems) = refs[:CHIPS], refs[CHIPS:]
    replica = lax.axis_index("dp")
    z_hi, y, core = replica // 8, (replica // 2) % 4, replica % 2
    loads = [pltpu.make_async_copy(piece, held.at[i], sems.at[i]) for i, piece in enumerate(pieces)]
    for load in loads:
        load.start()
    for index, (flip, turn) in enumerate(PIECE_FROM):
        chip = (z_hi if flip == 0 else 1 - z_hi) * 4 + (y + turn) % 4
        loads[index].wait()
        for start in range(0, D, COLS):
            part = slice(start, start + COLS)
            term = jnp.dot(grads[chip], held[index, :, part], preferred_element_type=jnp.float32)
            total[:, part] = term if index == 0 else total[:, part] + term
    for chip in range(CHIPS):
        turned = total[:, chip * WIDE : (chip + 1) * WIDE].T
        low, high = turned[:SHARE], turned[SHARE:]
        keep[chip] = jnp.where(core == 0, low, high)
        give[chip] = jnp.where(core == 0, high, low).astype(jnp.bfloat16)


def product(grads, pieces):
    block = (CHIPS, SHARE, WIDE)
    return pl.pallas_call(
        product_kernel,
        out_shape=[jax.ShapeDtypeStruct(block, jnp.float32), jax.ShapeDtypeStruct(block, jnp.bfloat16)],
        in_specs=[VM] + [ANY] * CHIPS,
        out_specs=[VM, VM],
        scratch_shapes=[
            pltpu.VMEM((CHIPS, SPAN, D), jnp.bfloat16),
            pltpu.VMEM((WIDE, D), jnp.float32),
            pltpu.SemaphoreType.DMA((CHIPS,)),
        ],
        name="weight_product",
        compiler_params=params(36),
    )(grads, *pieces)


def add_kernel(keep, taken, whole):
    whole[...] = (keep[...] + taken[...].astype(jnp.float32)).astype(jnp.bfloat16)


def add(keep, taken):
    return pl.pallas_call(
        add_kernel,
        out_shape=jax.ShapeDtypeStruct(taken.shape, taken.dtype),
        in_specs=[VM, VM],
        out_specs=VM,
        name="add_cores",
        compiler_params=params(24),
    )(keep, taken)


def finish_kernel(blocks, weight, gain, rows_ref, gain_ref, own, sem):
    start = pl.multiple_of(lax.axis_index("dp") * SHARE, SHARE)
    load = pltpu.make_async_copy(weight.at[pl.ds(start, SHARE)], own, sem)
    load.start()
    for chip in range(CHIPS):
        rows_ref[:, chip * WIDE : (chip + 1) * WIDE] = blocks[chip]
    load.wait()
    total = jnp.zeros((SHARE, 1), jnp.float32)
    for chip in range(CHIPS):
        part = slice(chip * WIDE, (chip + 1) * WIDE)
        term = own[:, part].astype(jnp.float32) * blocks[chip].astype(jnp.float32)
        total = total + jnp.sum(term, axis=-1, keepdims=True)
    gain_ref[...] = total


def finish(blocks, weight, gain):
    return pl.pallas_call(
        finish_kernel,
        out_shape=[
            jax.ShapeDtypeStruct((SHARE, D), jnp.bfloat16),
            jax.ShapeDtypeStruct((SHARE, 1), jnp.float32),
        ],
        in_specs=[VM, ANY, VM],
        out_specs=[VM, VM],
        scratch_shapes=[pltpu.VMEM((SHARE, D), jnp.bfloat16), pltpu.SemaphoreType.DMA],
        name="weight_rows",
        compiler_params=params(12),
    )(blocks, far(weight), gain)


PIECE_FROM = ((0, 0), (0, 3), (0, 1), (1, 0), (1, 3), (1, 1), (0, 2), (1, 2))


def along(flip, turn):
    pairs = []
    for replica in range(REPLICAS):
        z_hi, y, core = replica // 8, (replica // 2) % 4, replica % 2
        source = (z_hi ^ flip) * 8 + (y + turn) % 4 * 2 + core
        pairs.append((source, replica))
    return pairs


def bring(array, flip, turn):
    return lax.ppermute(array, "dp", along(flip, turn))


def on_device(tokens, cotangent, weights, gains):
    axes = ("chain", "dp")
    output, arena, saved = first(
        weights[0], tokens.reshape(SPAN, D), cotangent.reshape(SPAN, D), gains
    )
    arriving = [None] * STREAMS
    returning = [None] * STREAMS
    pieces = {}
    for moment in range(TURN + SLOTS):
        sent = list(arriving)
        for stream in range(STREAMS):
            if moment < LAST + SLOTS:
                if moment or stream:
                    output, arena, saved = forward(
                        moment, stream, arriving[stream], gains, arena, saved
                    )
                senders = [s for s in range(LAST) if 0 <= moment - s < SLOTS]
                if senders:
                    sent[stream] = lax.ppermute(output, axes, route(senders, True))
            if moment >= LAST:
                held = HELD.get((moment, stream), ())
                output, arena, *through = backward(
                    moment, stream, returning[stream], gains, arena, [pieces[name] for name in held],
                    (moment, stream) == (TURN + SLOTS - 1, STREAMS - 1),
                )
                pieces.update(zip(held, through))
                packed = through[-1:]
                senders = [s for s in range(1, SECTIONS) if 0 <= moment - TURN + s < SLOTS]
                if senders:
                    returning[stream] = lax.ppermute(output, axes, route(senders, False))
            if (moment, stream) == (LAST + SLOTS - 1, STREAMS - 1):
                pieces[0, 0] = saved
                pieces[1, 0] = bring(saved, 1, 0)
                pieces[0, 3] = bring(saved, 0, 3)
                pieces[0, 1] = bring(saved, 0, 1)
            if (moment, stream) == FLIPPED:
                pieces[1, 3] = bring(pieces[1, 0], 0, 3)
                pieces[1, 1] = bring(pieces[1, 0], 0, 1)
            if (moment, stream) == FAR:
                pieces[0, 2] = bring(pieces[0, 3], 0, 3)
                pieces[1, 2] = bring(pieces[1, 1], 0, 1)
        arriving = sent

    chips = [[replica for replica in range(REPLICAS) if replica % 2 == core] for core in range(2)]
    columns = lax.all_to_all(packed[0], "dp", 0, 0, axis_index_groups=chips)
    keep, give = product(columns, [pieces[name] for name in PIECE_FROM])
    other = [(replica ^ 1, replica) for replica in range(REPLICAS)]
    blocks = add(keep, lax.ppermute(give, "dp", other))
    blocks = lax.all_to_all(blocks, "dp", 0, 0, axis_index_groups=chips)
    weight_rows, sums = finish(blocks, weights[0], gains)
    own_gain = lax.dynamic_slice_in_dim(gains[0], lax.axis_index("dp") * SHARE, SHARE, 0)
    return (weight_rows[None], (sums[:, 0] / own_gain)[None])


FLIPPED = (LAST + SLOTS + 1, 1)
FAR = (LAST + SLOTS + 4, 1)
HELD = {FLIPPED: ((1, 0),), FAR: ((0, 3), (1, 1))}


def solution(mesh):
    placed = (P(None, "dp", None), P(None, "dp", None), P("chain", None, None), P("chain", None))
    return jax.shard_map(
        on_device,
        mesh=mesh,
        in_specs=placed,
        out_specs=(P("chain", "dp", None), P("chain", "dp")),
        check_vma=False,
    )
```

```python
import functools

import jax
import jax.numpy as jnp
from jax import lax
from jax.experimental import pallas as pl
from jax.experimental.pallas import tpu as pltpu
from jax.sharding import PartitionSpec as P

SECTIONS = 8
LAST = SECTIONS - 1
TURN = 2 * LAST
REPLICAS = 16
D = 3072
SPAN = 256
SHARE = D // REPLICAS
CHIPS = REPLICAS // 2
WIDE = D // CHIPS
STREAMS = 2
SLOTS = 2
ROWS = SPAN // (STREAMS * SLOTS)
COLS = 1024
PIECES = 6
PIECE = D // PIECES
TURNED = D
INPUT = 2 * D
GRAD = INPUT + SPAN
ENDS = GRAD + SPAN
HIGH = ENDS + SPAN
LOW = HIGH + SPAN
GAIN = LOW + SPAN
ARENA = GAIN + 16
HALF = SECTIONS // 2
SPLIT = HALF + SLOTS - 2
COST = pl.CostEstimate(flops=2 * ROWS * D * D, bytes_accessed=4 * D * D, transcendentals=0)
VM = pl.BlockSpec(memory_space=pltpu.VMEM)
ANY = pl.BlockSpec(memory_space=pl.ANY)


def pin(array):
    return pltpu.with_memory_space_constraint(array, pltpu.VMEM)


def far(array):
    return pltpu.with_memory_space_constraint(array, pltpu.HBM)


def params(mib):
    return pltpu.CompilerParams(vmem_limit_bytes=mib << 20)


def partner(section, replica):
    z_hi, rest = divmod(replica, 8)
    core = rest % 2
    if section % 2 == 0 and core == 1:
        z_hi = 1 - z_hi
    return z_hi * 8 + rest


def route(sections, forward):
    pairs = []
    for section in sections:
        low = section if forward else section - 1
        for replica in range(REPLICAS):
            here, there = low * REPLICAS + replica, (low + 1) * REPLICAS + partner(low, replica)
            pairs.append((here, there) if forward else (there, here))
    return pairs


def inverse_rms(x_float):
    return lax.rsqrt(jnp.mean(x_float * x_float, axis=-1, keepdims=True) + 1e-06)


def at_slot(base, slot):
    return pl.ds(pl.multiple_of(base + slot * ROWS, ROWS), ROWS)


def gain_of(arena, part):
    three = arena[GAIN : GAIN + 16, part].astype(jnp.float32)
    return three[0:1] + three[1:2] + three[2:3]


def each_part(body):
    def run(index, carry):
        body(index, pl.ds(pl.multiple_of(index * COLS, COLS), COLS))
        return carry

    lax.fori_loop(0, D // COLS, run, 0)


def forward_block(slot, given, arena, saved, output, scaled, sem, ready=None):
    arena[at_slot(INPUT, slot)] = given
    x_float = given.astype(jnp.float32)
    scaled[...] = (x_float * inverse_rms(x_float) * gain_of(arena, slice(None))).astype(jnp.bfloat16)
    saves = [pltpu.make_async_copy(scaled, a.at[at_slot(0, slot)], sem) for a in saved]
    if len(saves) == 1:
        saves[0].start()
    else:
        low = lax.axis_index("chain") < HALF
        pl.when(low)(saves[0].start)
        pl.when(jnp.logical_not(low))(saves[1].start)

    def column_part(index, part):
        if ready is not None:
            ready(index)
        hidden = jnp.dot(scaled[...], arena[0:D, part], preferred_element_type=jnp.float32)
        high = hidden.astype(jnp.bfloat16)
        arena[at_slot(HIGH, slot), part] = high
        arena[at_slot(LOW, slot), part] = (hidden - high.astype(jnp.float32)).astype(jnp.bfloat16)
        x_part = arena[at_slot(INPUT, slot), part].astype(jnp.float32)
        output[:, part] = (x_part + jax.nn.gelu(hidden)).astype(jnp.bfloat16)

    each_part(column_part)
    saves[0].wait()


def first_kernel(weight, tokens, cotangent, gain, output, arena, saved, scaled, made, gain_row, sem, loads):
    section = lax.axis_index("chain")
    ends = arena.at[pl.ds(ENDS, SPAN)]
    load_gain = pltpu.make_async_copy(gain, gain_row, loads.at[0])
    load_tokens = pltpu.make_async_copy(tokens, ends, loads.at[1])
    load_cotangent = pltpu.make_async_copy(cotangent, ends, loads.at[1])

    def load_part(index):
        part = pl.ds(pl.multiple_of(index * COLS, COLS), COLS)
        return pltpu.make_async_copy(weight.at[:, part], arena.at[pl.ds(0, D), part], loads.at[2 + index])

    load_gain.start()

    @pl.when(section == 0)
    def _():
        load_tokens.start()

    for index in range(D // COLS):
        load_part(index).start()

    @pl.when(section == LAST)
    def _():
        load_cotangent.start()

    load_gain.wait()
    row = gain_row[...]
    high = row.astype(jnp.bfloat16).astype(jnp.float32)
    middle = (row - high).astype(jnp.bfloat16).astype(jnp.float32)
    blank = jnp.zeros((13, D), jnp.float32)
    three = jnp.concatenate([high, middle, row - high - middle, blank], axis=0)
    arena[GAIN : GAIN + 16] = three.astype(jnp.bfloat16)

    @pl.when(section == 0)
    def _():
        load_tokens.wait()
        given = arena[ENDS : ENDS + ROWS]
        forward_block(0, given, arena, [saved], made, scaled, sem, lambda index: load_part(index).wait())
        pltpu.sync_copy(made, output)

    @pl.when(section != 0)
    def _():
        for index in range(D // COLS):
            load_part(index).wait()

    @pl.when(section == LAST)
    def _():
        load_cotangent.wait()


def first(weight, tokens, cotangent, gain):
    return pl.pallas_call(
        first_kernel,
        out_shape=[
            pltpu.HBM((ROWS, D), jnp.bfloat16),
            pltpu.VMEM((ARENA, D), jnp.bfloat16),
            pltpu.HBM((SPAN, D), jnp.bfloat16),
        ],
        in_specs=[ANY] * 4,
        out_specs=[ANY, VM, ANY],
        scratch_shapes=[
            pltpu.VMEM((ROWS, D), jnp.bfloat16),
            pltpu.VMEM((ROWS, D), jnp.bfloat16),
            pltpu.VMEM((1, D), jnp.float32),
            pltpu.SemaphoreType.DMA,
            pltpu.SemaphoreType.DMA((2 + D // COLS,)),
        ],
        name="load_and_first_block",
        cost_estimate=COST,
        compiler_params=params(6),
    )(far(weight), far(tokens), far(cotangent), far(gain))


def turn_piece(piece, arena):
    step = 256

    def run(index, carry):
        start = pl.multiple_of(piece * PIECE + index * step, step)
        arena[TURNED : TURNED + D, pl.ds(start, step)] = arena[pl.ds(start, step), :].T
        return carry

    lax.fori_loop(0, PIECE // step, run, 0)


def forward_kernel(moment, stream, old, *refs):
    given_ref = refs[0] if moment else None
    output, arena, *saves, scaled, sem = refs[int(moment > 0) + 1 + old :]
    section = lax.axis_index("chain")
    place = moment - section
    active = jnp.logical_and(place >= 0, place < SLOTS)

    @pl.when(active)
    def _():
        start = ENDS + (stream * SLOTS + moment) * ROWS
        if moment == 0:
            given = arena[start : start + ROWS]
        elif moment < SLOTS:
            given = jnp.where(section == 0, arena[start : start + ROWS], given_ref[...])
        else:
            given = given_ref[...]
        forward_block(stream * SLOTS + place, given, arena, saves, output, scaled, sem)

    if stream == STREAMS - 1 and moment < PIECES + SLOTS:
        piece = jnp.where(place < 0, moment, moment - SLOTS)

        @pl.when(jnp.logical_and(jnp.logical_not(active), piece < PIECES))
        def _():
            turn_piece(piece, arena)


def forward(moment, stream, given, arena, saved):
    given = [given] if moment else []
    low, high = saved
    old = ([low] if moment <= SPLIT else []) + ([high] if high is not None else [])
    count = 1 + len(given)
    new = int(moment == SPLIT and high is None)
    output, arena, *kept = pl.pallas_call(
        functools.partial(forward_kernel, moment, stream, len(old)),
        out_shape=[
            pltpu.VMEM((ROWS, D), jnp.bfloat16),
            jax.ShapeDtypeStruct(arena.shape, arena.dtype),
        ]
        + [pltpu.HBM((SPAN, D), jnp.bfloat16)] * (len(old) + new),
        in_specs=[VM] * count + [ANY] * len(old),
        out_specs=[VM, VM] + [ANY] * (len(old) + new),
        input_output_aliases={count - 1 + i: 1 + i for i in range(1 + len(old))},
        scratch_shapes=[pltpu.VMEM((ROWS, D), jnp.bfloat16), pltpu.SemaphoreType.DMA],
        name=f"forward_{moment}_{stream}",
        cost_estimate=COST,
        compiler_params=params(6),
    )(*given, pin(arena), *[far(a) for a in old])
    if moment <= SPLIT:
        low = kept.pop(0)
    return output, arena, (low, kept[0] if kept else None)


def backward_kernel(moment, stream, held, pack, *refs):
    given_ref = refs[0] if moment > LAST else None
    output, arena = refs[len(refs) - held - pack - 2 : len(refs) - held - pack]
    section = lax.axis_index("chain")
    place = moment - TURN + section
    slot = stream * SLOTS + place

    def upstream(part):
        start = ENDS + (stream * SLOTS + moment - LAST) * ROWS
        if moment == LAST:
            given = arena[start : start + ROWS, part]
        elif moment - LAST < SLOTS:
            given = jnp.where(section == LAST, arena[start : start + ROWS, part], given_ref[:, part])
        else:
            given = given_ref[:, part]
        return given.astype(jnp.float32)

    @pl.when(jnp.logical_and(place >= 0, place < SLOTS))
    def _():
        def gelu_part(index, total):
            part = pl.ds(pl.multiple_of(index * COLS, COLS), COLS)
            high = arena[at_slot(HIGH, slot), part].astype(jnp.float32)
            hidden = high + arena[at_slot(LOW, slot), part].astype(jnp.float32)
            _, pullback = jax.vjp(jax.nn.gelu, hidden)
            grad_hidden = pullback(upstream(part))[0].astype(jnp.bfloat16)
            arena[at_slot(GRAD, slot), part] = grad_hidden
            return total + jnp.sum(grad_hidden.astype(jnp.float32) * hidden, axis=-1, keepdims=True)

        total = lax.fori_loop(0, D // COLS, gelu_part, jnp.zeros((ROWS, 1), jnp.float32))
        if moment == TURN + SLOTS - 1:
            return

        @pl.when(section > 0)
        def _():
            inv_rms = inverse_rms(arena[at_slot(INPUT, slot)].astype(jnp.float32))
            mean = total * (1.0 / D)

            def column_part(index, part):
                grad_normed = gain_of(arena, part) * jnp.dot(
                    arena[at_slot(GRAD, slot)],
                    arena[TURNED : TURNED + D, part],
                    preferred_element_type=jnp.float32,
                )
                normed = arena[at_slot(INPUT, slot), part].astype(jnp.float32) * inv_rms
                grad_input = upstream(part) + inv_rms * (grad_normed - normed * mean)
                output[:, part] = grad_input.astype(jnp.bfloat16)

            each_part(column_part)

    if pack:
        packed = refs[-1]
        for chip in range(CHIPS):
            packed[chip] = arena[GRAD : GRAD + SPAN, chip * WIDE : (chip + 1) * WIDE].T


def backward(moment, stream, given, arena, held, pack):
    given = [given] if moment > LAST else []
    count = len(given)
    return pl.pallas_call(
        functools.partial(backward_kernel, moment, stream, len(held), int(pack)),
        out_shape=[
            jax.ShapeDtypeStruct((ROWS, D), jnp.bfloat16),
            jax.ShapeDtypeStruct(arena.shape, arena.dtype),
        ]
        + [pltpu.HBM(a.shape, a.dtype) for a in held]
        + [jax.ShapeDtypeStruct((CHIPS, WIDE, SPAN), jnp.bfloat16)] * pack,
        in_specs=[VM] * (1 + count) + [ANY] * len(held),
        out_specs=[VM, VM] + [ANY] * len(held) + [VM] * pack,
        input_output_aliases={count + i: 1 + i for i in range(1 + len(held))},
        name=f"backward_{moment}_{stream}",
        cost_estimate=COST,
        compiler_params=params(6),
    )(*given, pin(arena), *[far(a) for a in held])


def product_kernel(grads, *refs):
    pieces, (keep, give, held, total, sems) = refs[: 2 * CHIPS], refs[2 * CHIPS :]
    replica = lax.axis_index("dp")
    z_hi, y, core = replica // 8, (replica // 2) % 4, replica % 2
    low = lax.axis_index("chain") < HALF

    def load(index, half):
        return pltpu.make_async_copy(pieces[half * CHIPS + index], held.at[index], sems.at[index])

    for index in range(CHIPS):
        pl.when(low)(load(index, 0).start)
        pl.when(jnp.logical_not(low))(load(index, 1).start)
    for index, (flip, turn) in enumerate(PIECE_FROM):
        chip = (z_hi if flip == 0 else 1 - z_hi) * 4 + (y + turn) % 4
        load(index, 0).wait()

        def column_part(_, part, index=index, chip=chip):
            term = jnp.dot(grads[chip], held[index, :, part], preferred_element_type=jnp.float32)
            total[:, part] = term if index == 0 else total[:, part] + term

        each_part(column_part)

    def turn(chip, carry):
        turned = total[:, pl.ds(pl.multiple_of(chip * WIDE, WIDE), WIDE)].T
        low_rows, high_rows = turned[:SHARE], turned[SHARE:]
        keep[chip] = jnp.where(core == 0, low_rows, high_rows)
        give[chip] = jnp.where(core == 0, high_rows, low_rows).astype(jnp.bfloat16)
        return carry

    lax.fori_loop(0, CHIPS, turn, 0)


def product(grads, pieces):
    block = (CHIPS, SHARE, WIDE)
    return pl.pallas_call(
        product_kernel,
        out_shape=[jax.ShapeDtypeStruct(block, jnp.float32), jax.ShapeDtypeStruct(block, jnp.bfloat16)],
        in_specs=[VM] + [ANY] * len(pieces),
        out_specs=[VM, VM],
        scratch_shapes=[
            pltpu.VMEM((CHIPS, SPAN, D), jnp.bfloat16),
            pltpu.VMEM((WIDE, D), jnp.float32),
            pltpu.SemaphoreType.DMA((CHIPS,)),
        ],
        name="weight_product",
        compiler_params=params(36),
    )(grads, *[far(a) for a in pieces])


def add_kernel(keep, taken, whole):
    whole[...] = (keep[...] + taken[...].astype(jnp.float32)).astype(jnp.bfloat16)


def add(keep, taken):
    return pl.pallas_call(
        add_kernel,
        out_shape=jax.ShapeDtypeStruct(taken.shape, taken.dtype),
        in_specs=[VM, VM],
        out_specs=VM,
        name="add_cores",
        compiler_params=params(24),
    )(keep, taken)


def finish_kernel(blocks, weight, rows_ref, sums_ref, own, sem):
    start = pl.multiple_of(lax.axis_index("dp") * SHARE, SHARE)
    load = pltpu.make_async_copy(weight.at[pl.ds(start, SHARE)], own, sem)
    load.start()
    for chip in range(CHIPS):
        rows_ref[:, chip * WIDE : (chip + 1) * WIDE] = blocks[chip]
    load.wait()
    total = jnp.zeros((SHARE, 1), jnp.float32)
    for chip in range(CHIPS):
        part = slice(chip * WIDE, (chip + 1) * WIDE)
        term = own[:, part].astype(jnp.float32) * blocks[chip].astype(jnp.float32)
        total = total + jnp.sum(term, axis=-1, keepdims=True)
    sums_ref[...] = total


def finish(blocks, weight):
    return pl.pallas_call(
        finish_kernel,
        out_shape=[
            jax.ShapeDtypeStruct((SHARE, D), jnp.bfloat16),
            jax.ShapeDtypeStruct((SHARE, 1), jnp.float32),
        ],
        in_specs=[VM, ANY],
        out_specs=[VM, VM],
        scratch_shapes=[pltpu.VMEM((SHARE, D), jnp.bfloat16), pltpu.SemaphoreType.DMA],
        name="weight_rows",
        compiler_params=params(12),
    )(blocks, far(weight))


PIECE_FROM = ((0, 0), (0, 3), (0, 1), (1, 0), (1, 3), (1, 1), (0, 2), (1, 2))


def along(flip, turn):
    pairs = []
    for replica in range(REPLICAS):
        z_hi, y, core = replica // 8, (replica // 2) % 4, replica % 2
        source = (z_hi ^ flip) * 8 + (y + turn) % 4 * 2 + core
        pairs.append((source, replica))
    return pairs


def bring(array, flip, turn, half):
    pairs = [
        (section * REPLICAS + source, section * REPLICAS + target)
        for section in range(half * HALF, (half + 1) * HALF)
        for source, target in along(flip, turn)
    ]
    return lax.ppermute(array, ("chain", "dp"), pairs)


GATHER = (
    {(5, 1): 0, (7, 0): 1, (8, 1): 2, (9, 1): 3},
    {(11, 1): 0, (13, 0): 1, (14, 0): 2, (15, 0): 3},
)
SOURCES = (((0, 0),), ((0, 3),), ((1, 0),), ((1, 1),))


def gather(stage, pieces, half):
    if stage == 0:
        pieces[1, 0] = bring(pieces[0, 0], 1, 0, half)
    if stage in (0, 2):
        flip = stage // 2
        pieces[flip, 3] = bring(pieces[flip, 0], 0, 3, half)
        pieces[flip, 1] = bring(pieces[flip, 0], 0, 1, half)
    if stage == 1:
        pieces[0, 2] = bring(pieces[0, 3], 0, 3, half)
    if stage == 3:
        pieces[1, 2] = bring(pieces[1, 1], 0, 1, half)


def on_device(tokens, cotangent, weights, gains):
    axes = ("chain", "dp")
    output, arena, low = first(
        weights[0], tokens.reshape(SPAN, D), cotangent.reshape(SPAN, D), gains
    )
    saved = (low, None)
    arriving = [None] * STREAMS
    returning = [None] * STREAMS
    pieces = ({}, {})
    for moment in range(TURN + SLOTS):
        sent = list(arriving)
        for stream in range(STREAMS):
            now = (moment, stream)
            if moment < LAST + SLOTS:
                if moment or stream:
                    output, arena, saved = forward(moment, stream, arriving[stream], arena, saved)
                senders = [s for s in range(LAST) if 0 <= moment // 2 * 2 + 1 - s < SLOTS + 1]
                if moment < LAST + SLOTS - 1:
                    sent[stream] = lax.ppermute(output, axes, route(senders, True))
                if now == (SPLIT, STREAMS - 1):
                    pieces[0][0, 0] = saved[0]
                if now == (LAST + SLOTS - 1, STREAMS - 1):
                    pieces[1][0, 0] = saved[1]
            if moment >= LAST:
                held = [
                    (half, name)
                    for half in range(2)
                    if now in GATHER[half]
                    for name in SOURCES[GATHER[half][now]]
                ]
                output, arena, *through = backward(
                    moment, stream, returning[stream], arena,
                    [pieces[half][name] for half, name in held],
                    now == (TURN + SLOTS - 1, STREAMS - 1),
                )
                for (half, name), array in zip(held, through):
                    pieces[half][name] = array
                late = LAST + (moment - LAST) // 2 * 2 + 1
                senders = [s for s in range(1, SECTIONS) if 0 <= late - TURN + s < SLOTS + 1]
                if moment < TURN + SLOTS - 1:
                    returning[stream] = lax.ppermute(output, axes, route(senders, False))
            for half in range(2):
                if now in GATHER[half]:
                    gather(GATHER[half][now], pieces[half], half)
        arriving = sent

    chips = [[replica for replica in range(REPLICAS) if replica % 2 == core] for core in range(2)]
    columns = lax.all_to_all(through[-1], "dp", 0, 0, axis_index_groups=chips)
    keep, give = product(columns, [pieces[half][name] for half in range(2) for name in PIECE_FROM])
    other = [(replica ^ 1, replica) for replica in range(REPLICAS)]
    blocks = add(keep, lax.ppermute(give, "dp", other))
    blocks = lax.all_to_all(blocks, "dp", 0, 0, axis_index_groups=chips)
    weight_rows, sums = finish(blocks, weights[0])
    own_gain = lax.dynamic_slice_in_dim(gains[0], lax.axis_index("dp") * SHARE, SHARE, 0)
    return (weight_rows[None], (sums[:, 0] / own_gain)[None])


def solution(mesh):
    placed = (P(None, "dp", None), P(None, "dp", None), P("chain", None, None), P("chain", None))
    return jax.shard_map(
        on_device,
        mesh=mesh,
        in_specs=placed,
        out_specs=(P("chain", "dp", None), P("chain", "dp")),
        check_vma=False,
    )
```

```python
import functools

import jax
import jax.numpy as jnp
from jax import lax
from jax.experimental import pallas as pl
from jax.experimental.pallas import tpu as pltpu
from jax.sharding import PartitionSpec as P

SECTIONS = 8
LAST = SECTIONS - 1
TURN = 2 * LAST
REPLICAS = 16
D = 3072
SPAN = 256
SHARE = D // REPLICAS
CHIPS = REPLICAS // 2
WIDE = D // CHIPS
STREAMS = 2
SLOTS = 2
ROWS = SPAN // (STREAMS * SLOTS)
COLS = 1024
PIECES = 6
PIECE = D // PIECES
TURNED = D
INPUT = 2 * D
GRAD = INPUT + SPAN
ENDS = GRAD + SPAN
HIGH = ENDS + SPAN
LOW = HIGH + SPAN
GAIN = LOW + SPAN
ARENA = GAIN + 16
HALF = SECTIONS // 2
SPLIT = HALF + SLOTS - 2
CROSSING = (7, 8)
PLAIN = 20
CROSSED = 1
VM = pl.BlockSpec(memory_space=pltpu.VMEM)
ANY = pl.BlockSpec(memory_space=pl.ANY)


def cost(moment):
    weight = CROSSED if moment in CROSSING else PLAIN
    return pl.CostEstimate(flops=weight * 2 * ROWS * D * D, bytes_accessed=4 * D * D, transcendentals=0)


def pin(array):
    return pltpu.with_memory_space_constraint(array, pltpu.VMEM)


def far(array):
    return pltpu.with_memory_space_constraint(array, pltpu.HBM)


def params(mib):
    return pltpu.CompilerParams(vmem_limit_bytes=mib << 20)


def partner(section, replica):
    z_hi, rest = divmod(replica, 8)
    core = rest % 2
    if section % 2 == 0 and core == 1:
        z_hi = 1 - z_hi
    return z_hi * 8 + rest


def route(sections, forward):
    pairs = []
    for section in sections:
        low = section if forward else section - 1
        for replica in range(REPLICAS):
            here, there = low * REPLICAS + replica, (low + 1) * REPLICAS + partner(low, replica)
            pairs.append((here, there) if forward else (there, here))
    return pairs


def inverse_rms(x_float):
    return lax.rsqrt(jnp.mean(x_float * x_float, axis=-1, keepdims=True) + 1e-06)


def at_slot(base, slot):
    return pl.ds(pl.multiple_of(base + slot * ROWS, ROWS), ROWS)


def gain_of(arena, part):
    three = arena[GAIN : GAIN + 16, part].astype(jnp.float32)
    return three[0:1] + three[1:2] + three[2:3]


def each_part(body):
    def run(index, carry):
        body(index, pl.ds(pl.multiple_of(index * COLS, COLS), COLS))
        return carry

    lax.fori_loop(0, D // COLS, run, 0)


def forward_block(slot, given, arena, saved, output, scaled, sem, ready=None):
    arena[at_slot(INPUT, slot)] = given
    x_float = given.astype(jnp.float32)
    scaled[...] = (x_float * inverse_rms(x_float) * gain_of(arena, slice(None))).astype(jnp.bfloat16)
    saves = [pltpu.make_async_copy(scaled, a.at[at_slot(0, slot)], sem) for a in saved]
    if len(saves) == 1:
        saves[0].start()
    else:
        low = lax.axis_index("chain") < HALF
        pl.when(low)(saves[0].start)
        pl.when(jnp.logical_not(low))(saves[1].start)

    def column_part(index, part):
        if ready is not None:
            ready(index)
        hidden = jnp.dot(scaled[...], arena[0:D, part], preferred_element_type=jnp.float32)
        high = hidden.astype(jnp.bfloat16)
        arena[at_slot(HIGH, slot), part] = high
        arena[at_slot(LOW, slot), part] = (hidden - high.astype(jnp.float32)).astype(jnp.bfloat16)
        x_part = arena[at_slot(INPUT, slot), part].astype(jnp.float32)
        output[:, part] = (x_part + jax.nn.gelu(hidden)).astype(jnp.bfloat16)

    each_part(column_part)
    saves[0].wait()


def first_kernel(weight, tokens, cotangent, gain, output, arena, saved, scaled, made, gain_row, sem, loads):
    section = lax.axis_index("chain")
    ends = arena.at[pl.ds(ENDS, SPAN)]
    load_gain = pltpu.make_async_copy(gain, gain_row, loads.at[0])
    load_tokens = pltpu.make_async_copy(tokens, ends, loads.at[1])
    load_cotangent = pltpu.make_async_copy(cotangent, ends, loads.at[1])

    def load_part(index):
        part = pl.ds(pl.multiple_of(index * COLS, COLS), COLS)
        return pltpu.make_async_copy(weight.at[:, part], arena.at[pl.ds(0, D), part], loads.at[2 + index])

    load_gain.start()

    @pl.when(section == 0)
    def _():
        load_tokens.start()

    for index in range(D // COLS):
        load_part(index).start()

    @pl.when(section == LAST)
    def _():
        load_cotangent.start()

    load_gain.wait()
    row = gain_row[...]
    high = row.astype(jnp.bfloat16).astype(jnp.float32)
    middle = (row - high).astype(jnp.bfloat16).astype(jnp.float32)
    blank = jnp.zeros((13, D), jnp.float32)
    three = jnp.concatenate([high, middle, row - high - middle, blank], axis=0)
    arena[GAIN : GAIN + 16] = three.astype(jnp.bfloat16)

    @pl.when(section == 0)
    def _():
        load_tokens.wait()
        given = arena[ENDS : ENDS + ROWS]
        forward_block(0, given, arena, [saved], made, scaled, sem, lambda index: load_part(index).wait())
        pltpu.sync_copy(made, output)

    @pl.when(section != 0)
    def _():
        for index in range(D // COLS):
            load_part(index).wait()

    @pl.when(section == LAST)
    def _():
        load_cotangent.wait()


def first(weight, tokens, cotangent, gain):
    return pl.pallas_call(
        first_kernel,
        out_shape=[
            pltpu.HBM((ROWS, D), jnp.bfloat16),
            pltpu.VMEM((ARENA, D), jnp.bfloat16),
            pltpu.HBM((SPAN, D), jnp.bfloat16),
        ],
        in_specs=[ANY] * 4,
        out_specs=[ANY, VM, ANY],
        scratch_shapes=[
            pltpu.VMEM((ROWS, D), jnp.bfloat16),
            pltpu.VMEM((ROWS, D), jnp.bfloat16),
            pltpu.VMEM((1, D), jnp.float32),
            pltpu.SemaphoreType.DMA,
            pltpu.SemaphoreType.DMA((2 + D // COLS,)),
        ],
        name="load_and_first_block",
        cost_estimate=cost(0),
        compiler_params=params(6),
    )(far(weight), far(tokens), far(cotangent), far(gain))


def turn_piece(piece, arena):
    step = 256

    def run(index, carry):
        start = pl.multiple_of(piece * PIECE + index * step, step)
        arena[TURNED : TURNED + D, pl.ds(start, step)] = arena[pl.ds(start, step), :].T
        return carry

    lax.fori_loop(0, PIECE // step, run, 0)


def forward_kernel(moment, stream, old, *refs):
    given_ref = refs[0] if moment else None
    output, arena, *saves, scaled, sem = refs[int(moment > 0) + 1 + old :]
    section = lax.axis_index("chain")
    place = moment - section
    active = jnp.logical_and(place >= 0, place < SLOTS)

    @pl.when(active)
    def _():
        start = ENDS + (stream * SLOTS + moment) * ROWS
        if moment == 0:
            given = arena[start : start + ROWS]
        elif moment < SLOTS:
            given = jnp.where(section == 0, arena[start : start + ROWS], given_ref[...])
        else:
            given = given_ref[...]
        forward_block(stream * SLOTS + place, given, arena, saves, output, scaled, sem)

    if stream == STREAMS - 1 and moment < PIECES + SLOTS:
        piece = jnp.where(place < 0, moment, moment - SLOTS)

        @pl.when(jnp.logical_and(jnp.logical_not(active), piece < PIECES))
        def _():
            turn_piece(piece, arena)


def forward(moment, stream, given, arena, saved):
    given = [given] if moment else []
    low, high = saved
    old = ([low] if moment <= SPLIT else []) + ([high] if high is not None else [])
    count = 1 + len(given)
    new = int(moment == SPLIT and high is None)
    output, arena, *kept = pl.pallas_call(
        functools.partial(forward_kernel, moment, stream, len(old)),
        out_shape=[
            pltpu.VMEM((ROWS, D), jnp.bfloat16),
            jax.ShapeDtypeStruct(arena.shape, arena.dtype),
        ]
        + [pltpu.HBM((SPAN, D), jnp.bfloat16)] * (len(old) + new),
        in_specs=[VM] * count + [ANY] * len(old),
        out_specs=[VM, VM] + [ANY] * (len(old) + new),
        input_output_aliases={count - 1 + i: 1 + i for i in range(1 + len(old))},
        scratch_shapes=[pltpu.VMEM((ROWS, D), jnp.bfloat16), pltpu.SemaphoreType.DMA],
        name=f"forward_{moment}_{stream}",
        cost_estimate=cost(moment),
        compiler_params=params(6),
    )(*given, pin(arena), *[far(a) for a in old])
    if moment <= SPLIT:
        low = kept.pop(0)
    return output, arena, (low, kept[0] if kept else None)


def backward_kernel(moment, stream, held, pack, *refs):
    given_ref = refs[0] if moment > LAST else None
    output, arena = refs[len(refs) - held - pack - 2 : len(refs) - held - pack]
    section = lax.axis_index("chain")
    place = moment - TURN + section
    slot = stream * SLOTS + place

    def upstream(part):
        start = ENDS + (stream * SLOTS + moment - LAST) * ROWS
        if moment == LAST:
            given = arena[start : start + ROWS, part]
        elif moment - LAST < SLOTS:
            given = jnp.where(section == LAST, arena[start : start + ROWS, part], given_ref[:, part])
        else:
            given = given_ref[:, part]
        return given.astype(jnp.float32)

    @pl.when(jnp.logical_and(place >= 0, place < SLOTS))
    def _():
        def gelu_part(index, total):
            part = pl.ds(pl.multiple_of(index * COLS, COLS), COLS)
            high = arena[at_slot(HIGH, slot), part].astype(jnp.float32)
            hidden = high + arena[at_slot(LOW, slot), part].astype(jnp.float32)
            _, pullback = jax.vjp(jax.nn.gelu, hidden)
            grad_hidden = pullback(upstream(part))[0].astype(jnp.bfloat16)
            arena[at_slot(GRAD, slot), part] = grad_hidden
            return total + jnp.sum(grad_hidden.astype(jnp.float32) * hidden, axis=-1, keepdims=True)

        total = lax.fori_loop(0, D // COLS, gelu_part, jnp.zeros((ROWS, 1), jnp.float32))
        if moment == TURN + SLOTS - 1:
            return

        @pl.when(section > 0)
        def _():
            inv_rms = inverse_rms(arena[at_slot(INPUT, slot)].astype(jnp.float32))
            mean = total * (1.0 / D)

            def column_part(index, part):
                grad_normed = gain_of(arena, part) * jnp.dot(
                    arena[at_slot(GRAD, slot)],
                    arena[TURNED : TURNED + D, part],
                    preferred_element_type=jnp.float32,
                )
                normed = arena[at_slot(INPUT, slot), part].astype(jnp.float32) * inv_rms
                grad_input = upstream(part) + inv_rms * (grad_normed - normed * mean)
                output[:, part] = grad_input.astype(jnp.bfloat16)

            each_part(column_part)

    if pack:
        packed = refs[-1]
        for chip in range(CHIPS):
            packed[chip] = arena[GRAD : GRAD + SPAN, chip * WIDE : (chip + 1) * WIDE].T


def backward(moment, stream, given, arena, held, pack):
    given = [given] if moment > LAST else []
    count = len(given)
    return pl.pallas_call(
        functools.partial(backward_kernel, moment, stream, len(held), int(pack)),
        out_shape=[
            jax.ShapeDtypeStruct((ROWS, D), jnp.bfloat16),
            jax.ShapeDtypeStruct(arena.shape, arena.dtype),
        ]
        + [pltpu.HBM(a.shape, a.dtype) for a in held]
        + [jax.ShapeDtypeStruct((CHIPS, WIDE, SPAN), jnp.bfloat16)] * pack,
        in_specs=[VM] * (1 + count) + [ANY] * len(held),
        out_specs=[VM, VM] + [ANY] * len(held) + [VM] * pack,
        input_output_aliases={count + i: 1 + i for i in range(1 + len(held))},
        name=f"backward_{moment}_{stream}",
        cost_estimate=cost(moment),
        compiler_params=params(6),
    )(*given, pin(arena), *[far(a) for a in held])


def product_kernel(grads, *refs):
    pieces, (keep, give, held, turned_grads, total, sems) = refs[: 2 * CHIPS], refs[2 * CHIPS :]
    replica = lax.axis_index("dp")
    z_hi, y, core = replica // 8, (replica // 2) % 4, replica % 2
    low = lax.axis_index("chain") < HALF
    chips = [(z_hi if flip == 0 else 1 - z_hi) * 4 + (y + turn) % 4 for flip, turn in PIECE_FROM]

    def load(index, half, column):
        start = pl.multiple_of(chips[index] * SPAN, SPAN)
        part = pl.ds(column * COLS, COLS)
        return pltpu.make_async_copy(
            pieces[half * CHIPS + index].at[:, part], held.at[pl.ds(start, SPAN), part], sems.at[column]
        )

    for column in range(D // COLS):
        for index in range(CHIPS):
            pl.when(low)(load(index, 0, column).start)
            pl.when(jnp.logical_not(low))(load(index, 1, column).start)
    for chip in range(CHIPS):
        turned_grads[:, chip * SPAN : (chip + 1) * SPAN] = grads[chip]
    for column in range(D // COLS):
        part = slice(column * COLS, (column + 1) * COLS)
        pltpu.make_async_copy(held.at[:, part], held.at[:, part], sems.at[column]).wait()
        total[:, part] = jnp.dot(turned_grads[...], held[:, part], preferred_element_type=jnp.float32)

    def turn(chip, carry):
        turned = total[:, pl.ds(pl.multiple_of(chip * WIDE, WIDE), WIDE)].T
        low_rows, high_rows = turned[:SHARE], turned[SHARE:]
        keep[chip] = jnp.where(core == 0, low_rows, high_rows)
        give[chip] = jnp.where(core == 0, high_rows, low_rows).astype(jnp.bfloat16)
        return carry

    lax.fori_loop(0, CHIPS, turn, 0)


def product(grads, pieces):
    block = (CHIPS, SHARE, WIDE)
    return pl.pallas_call(
        product_kernel,
        out_shape=[jax.ShapeDtypeStruct(block, jnp.float32), jax.ShapeDtypeStruct(block, jnp.bfloat16)],
        in_specs=[VM] + [ANY] * len(pieces),
        out_specs=[VM, VM],
        scratch_shapes=[
            pltpu.VMEM((CHIPS * SPAN, D), jnp.bfloat16),
            pltpu.VMEM((WIDE, CHIPS * SPAN), jnp.bfloat16),
            pltpu.VMEM((WIDE, D), jnp.float32),
            pltpu.SemaphoreType.DMA((D // COLS,)),
        ],
        name="weight_product",
        compiler_params=params(36),
    )(grads, *[far(a) for a in pieces])


def add_kernel(keep, taken, whole):
    whole[...] = (keep[...] + taken[...].astype(jnp.float32)).astype(jnp.bfloat16)


def add(keep, taken):
    return pl.pallas_call(
        add_kernel,
        out_shape=jax.ShapeDtypeStruct(taken.shape, taken.dtype),
        in_specs=[VM, VM],
        out_specs=VM,
        name="add_cores",
        compiler_params=params(24),
    )(keep, taken)


def finish_kernel(blocks, weight, rows_ref, sums_ref, own, sem):
    start = pl.multiple_of(lax.axis_index("dp") * SHARE, SHARE)
    load = pltpu.make_async_copy(weight.at[pl.ds(start, SHARE)], own, sem)
    load.start()
    for chip in range(CHIPS):
        rows_ref[:, chip * WIDE : (chip + 1) * WIDE] = blocks[chip]
    load.wait()
    total = jnp.zeros((SHARE, 1), jnp.float32)
    for chip in range(CHIPS):
        part = slice(chip * WIDE, (chip + 1) * WIDE)
        term = own[:, part].astype(jnp.float32) * blocks[chip].astype(jnp.float32)
        total = total + jnp.sum(term, axis=-1, keepdims=True)
    sums_ref[...] = total


def finish(blocks, weight):
    return pl.pallas_call(
        finish_kernel,
        out_shape=[
            jax.ShapeDtypeStruct((SHARE, D), jnp.bfloat16),
            jax.ShapeDtypeStruct((SHARE, 1), jnp.float32),
        ],
        in_specs=[VM, ANY],
        out_specs=[VM, VM],
        scratch_shapes=[pltpu.VMEM((SHARE, D), jnp.bfloat16), pltpu.SemaphoreType.DMA],
        name="weight_rows",
        compiler_params=params(12),
    )(blocks, far(weight))


PIECE_FROM = ((0, 0), (0, 3), (0, 1), (1, 0), (1, 3), (1, 1), (0, 2), (1, 2))


def along(flip, turn):
    pairs = []
    for replica in range(REPLICAS):
        z_hi, y, core = replica // 8, (replica // 2) % 4, replica % 2
        source = (z_hi ^ flip) * 8 + (y + turn) % 4 * 2 + core
        pairs.append((source, replica))
    return pairs


def bring(array, flip, turn, half):
    pairs = [
        (section * REPLICAS + source, section * REPLICAS + target)
        for section in range(half * HALF, (half + 1) * HALF)
        for source, target in along(flip, turn)
    ]
    return lax.ppermute(array, ("chain", "dp"), pairs)


GATHER = (
    {(4, 1): 0, (9, 0): 1, (9, 1): 2, (10, 1): 3},
    {(11, 1): 0, (13, 0): 1, (13, 1): 2, (15, 0): 3},
)
SOURCES = (((0, 0),), ((0, 3),), ((1, 0),), ((1, 1),))


def gather(stage, pieces, half):
    if stage == 0:
        pieces[1, 0] = bring(pieces[0, 0], 1, 0, half)
    if stage in (0, 2):
        flip = stage // 2
        pieces[flip, 3] = bring(pieces[flip, 0], 0, 3, half)
        pieces[flip, 1] = bring(pieces[flip, 0], 0, 1, half)
    if stage == 1:
        pieces[0, 2] = bring(pieces[0, 3], 0, 3, half)
    if stage == 3:
        pieces[1, 2] = bring(pieces[1, 1], 0, 1, half)


def on_device(tokens, cotangent, weights, gains):
    axes = ("chain", "dp")
    output, arena, low = first(
        weights[0], tokens.reshape(SPAN, D), cotangent.reshape(SPAN, D), gains
    )
    saved = (low, None)
    arriving = [None] * STREAMS
    returning = [None] * STREAMS
    pieces = ({}, {})
    for moment in range(TURN + SLOTS):
        sent = list(arriving)
        for stream in range(STREAMS):
            now = (moment, stream)
            if moment < LAST + SLOTS:
                if moment or stream:
                    output, arena, saved = forward(moment, stream, arriving[stream], arena, saved)
                senders = [s for s in range(LAST) if 0 <= moment // 2 * 2 + 1 - s < SLOTS + 1]
                if moment < LAST + SLOTS - 1:
                    sent[stream] = lax.ppermute(output, axes, route(senders, True))
                if now == (SPLIT, STREAMS - 1):
                    pieces[0][0, 0] = saved[0]
                if now == (LAST + SLOTS - 1, STREAMS - 1):
                    pieces[1][0, 0] = saved[1]
            if moment >= LAST:
                held = [
                    (half, name)
                    for half in range(2)
                    if now in GATHER[half]
                    for name in SOURCES[GATHER[half][now]]
                ]
                output, arena, *through = backward(
                    moment, stream, returning[stream], arena,
                    [pieces[half][name] for half, name in held],
                    now == (TURN + SLOTS - 1, STREAMS - 1),
                )
                for (half, name), array in zip(held, through):
                    pieces[half][name] = array
                late = LAST + (moment - LAST) // 2 * 2 + 1
                senders = [s for s in range(1, SECTIONS) if 0 <= late - TURN + s < SLOTS + 1]
                if moment < TURN + SLOTS - 1:
                    returning[stream] = lax.ppermute(output, axes, route(senders, False))
            for half in range(2):
                if now in GATHER[half]:
                    gather(GATHER[half][now], pieces[half], half)
        arriving = sent

    chips = [[replica for replica in range(REPLICAS) if replica % 2 == core] for core in range(2)]
    columns = lax.all_to_all(through[-1], "dp", 0, 0, axis_index_groups=chips)
    keep, give = product(columns, [pieces[half][name] for half in range(2) for name in PIECE_FROM])
    other = [(replica ^ 1, replica) for replica in range(REPLICAS)]
    blocks = add(keep, lax.ppermute(give, "dp", other))
    blocks = lax.all_to_all(blocks, "dp", 0, 0, axis_index_groups=chips)
    weight_rows, sums = finish(blocks, weights[0])
    own_gain = lax.dynamic_slice_in_dim(gains[0], lax.axis_index("dp") * SHARE, SHARE, 0)
    return (weight_rows[None], (sums[:, 0] / own_gain)[None])


def solution(mesh):
    placed = (P(None, "dp", None), P(None, "dp", None), P("chain", None, None), P("chain", None))
    return jax.shard_map(
        on_device,
        mesh=mesh,
        in_specs=placed,
        out_specs=(P("chain", "dp", None), P("chain", "dp")),
        check_vma=False,
    )
```

```python
import functools

import jax
import jax.numpy as jnp
from jax import lax
from jax.experimental import pallas as pl
from jax.experimental.pallas import tpu as pltpu
from jax.sharding import PartitionSpec as P

SECTIONS = 8
LAST = SECTIONS - 1
TURN = 2 * LAST
REPLICAS = 16
D = 3072
SPAN = 256
SHARE = D // REPLICAS
CHIPS = REPLICAS // 2
WIDE = D // CHIPS
STREAMS = 2
SLOTS = 2
ROWS = SPAN // (STREAMS * SLOTS)
COLS = 1024
PIECES = 6
PIECE = D // PIECES
TURNED = D
INPUT = 2 * D
GRAD = INPUT + SPAN
ENDS = GRAD + SPAN
HIGH = ENDS + SPAN
LOW = HIGH + SPAN
GAIN = LOW + SPAN
ARENA = GAIN + 16
HALF = SECTIONS // 2
SPLIT = HALF + SLOTS - 2
WEIGHTS = {7: 0, 8: 0, 9: 1, 10: 1, 11: 1}
VM = pl.BlockSpec(memory_space=pltpu.VMEM)
ANY = pl.BlockSpec(memory_space=pl.ANY)


def cost(moment):
    weight = WEIGHTS.get(moment, 20)
    return pl.CostEstimate(flops=weight * 2 * ROWS * D * D, bytes_accessed=4 * D * D, transcendentals=0)


def pin(array):
    return pltpu.with_memory_space_constraint(array, pltpu.VMEM)


def far(array):
    return pltpu.with_memory_space_constraint(array, pltpu.HBM)


def params(mib):
    return pltpu.CompilerParams(vmem_limit_bytes=mib << 20)


def partner(section, replica):
    z_hi, rest = divmod(replica, 8)
    core = rest % 2
    if section % 2 == 0 and core == 1:
        z_hi = 1 - z_hi
    return z_hi * 8 + rest


def route(sections, forward):
    pairs = []
    for section in sections:
        low = section if forward else section - 1
        for replica in range(REPLICAS):
            here, there = low * REPLICAS + replica, (low + 1) * REPLICAS + partner(low, replica)
            pairs.append((here, there) if forward else (there, here))
    return pairs


def inverse_rms(x_float):
    return lax.rsqrt(jnp.mean(x_float * x_float, axis=-1, keepdims=True) + 1e-06)


def at_slot(base, slot):
    return pl.ds(pl.multiple_of(base + slot * ROWS, ROWS), ROWS)


def gain_of(arena, part):
    three = arena[GAIN : GAIN + 16, part].astype(jnp.float32)
    return three[0:1] + three[1:2] + three[2:3]


def each_part(body):
    def run(index, carry):
        body(index, pl.ds(pl.multiple_of(index * COLS, COLS), COLS))
        return carry

    lax.fori_loop(0, D // COLS, run, 0)


def forward_block(slot, given, arena, saved, output, scaled, sem, ready=None):
    arena[at_slot(INPUT, slot)] = given
    x_float = given.astype(jnp.float32)
    scaled[...] = (x_float * inverse_rms(x_float) * gain_of(arena, slice(None))).astype(jnp.bfloat16)
    saves = [pltpu.make_async_copy(scaled, a.at[at_slot(0, slot)], sem) for a in saved]
    if len(saves) == 1:
        saves[0].start()
    else:
        low = lax.axis_index("chain") < HALF
        pl.when(low)(saves[0].start)
        pl.when(jnp.logical_not(low))(saves[1].start)

    def column_part(index, part):
        if ready is not None:
            ready(index)
        hidden = jnp.dot(scaled[...], arena[0:D, part], preferred_element_type=jnp.float32)
        high = hidden.astype(jnp.bfloat16)
        arena[at_slot(HIGH, slot), part] = high
        arena[at_slot(LOW, slot), part] = (hidden - high.astype(jnp.float32)).astype(jnp.bfloat16)
        x_part = arena[at_slot(INPUT, slot), part].astype(jnp.float32)
        output[:, part] = (x_part + jax.nn.gelu(hidden)).astype(jnp.bfloat16)

    each_part(column_part)
    saves[0].wait()


def first_kernel(weight, tokens, cotangent, gain, output, arena, saved, scaled, made, gain_row, sem, loads):
    section = lax.axis_index("chain")
    ends = arena.at[pl.ds(ENDS, SPAN)]
    load_gain = pltpu.make_async_copy(gain, gain_row, loads.at[0])
    load_tokens = pltpu.make_async_copy(tokens, ends, loads.at[1])
    load_cotangent = pltpu.make_async_copy(cotangent, ends, loads.at[1])

    def load_part(index):
        part = pl.ds(pl.multiple_of(index * COLS, COLS), COLS)
        return pltpu.make_async_copy(weight.at[:, part], arena.at[pl.ds(0, D), part], loads.at[2 + index])

    load_gain.start()

    @pl.when(section == 0)
    def _():
        load_tokens.start()

    for index in range(D // COLS):
        load_part(index).start()

    @pl.when(section == LAST)
    def _():
        load_cotangent.start()

    load_gain.wait()
    row = gain_row[...]
    high = row.astype(jnp.bfloat16).astype(jnp.float32)
    middle = (row - high).astype(jnp.bfloat16).astype(jnp.float32)
    blank = jnp.zeros((13, D), jnp.float32)
    three = jnp.concatenate([high, middle, row - high - middle, blank], axis=0)
    arena[GAIN : GAIN + 16] = three.astype(jnp.bfloat16)

    @pl.when(section == 0)
    def _():
        load_tokens.wait()
        given = arena[ENDS : ENDS + ROWS]
        forward_block(0, given, arena, [saved], made, scaled, sem, lambda index: load_part(index).wait())
        pltpu.sync_copy(made, output)

    @pl.when(section != 0)
    def _():
        for index in range(D // COLS):
            load_part(index).wait()

    @pl.when(section == LAST)
    def _():
        load_cotangent.wait()


def first(weight, tokens, cotangent, gain):
    return pl.pallas_call(
        first_kernel,
        out_shape=[
            pltpu.HBM((ROWS, D), jnp.bfloat16),
            pltpu.VMEM((ARENA, D), jnp.bfloat16),
            pltpu.HBM((SPAN, D), jnp.bfloat16),
        ],
        in_specs=[ANY] * 4,
        out_specs=[ANY, VM, ANY],
        scratch_shapes=[
            pltpu.VMEM((ROWS, D), jnp.bfloat16),
            pltpu.VMEM((ROWS, D), jnp.bfloat16),
            pltpu.VMEM((1, D), jnp.float32),
            pltpu.SemaphoreType.DMA,
            pltpu.SemaphoreType.DMA((2 + D // COLS,)),
        ],
        name="load_and_first_block",
        cost_estimate=cost(0),
        compiler_params=params(6),
    )(far(weight), far(tokens), far(cotangent), far(gain))


def turn_piece(piece, arena):
    step = 256

    def run(index, carry):
        start = pl.multiple_of(piece * PIECE + index * step, step)
        arena[TURNED : TURNED + D, pl.ds(start, step)] = arena[pl.ds(start, step), :].T
        return carry

    lax.fori_loop(0, PIECE // step, run, 0)


def forward_kernel(moment, stream, old, *refs):
    given_ref = refs[0] if moment else None
    output, arena, *saves, scaled, sem = refs[int(moment > 0) + 1 + old :]
    section = lax.axis_index("chain")
    place = moment - section
    active = jnp.logical_and(place >= 0, place < SLOTS)

    @pl.when(active)
    def _():
        start = ENDS + (stream * SLOTS + moment) * ROWS
        if moment == 0:
            given = arena[start : start + ROWS]
        elif moment < SLOTS:
            given = jnp.where(section == 0, arena[start : start + ROWS], given_ref[...])
        else:
            given = given_ref[...]
        forward_block(stream * SLOTS + place, given, arena, saves, output, scaled, sem)

    if stream == STREAMS - 1 and moment < PIECES + SLOTS:
        piece = jnp.where(place < 0, moment, moment - SLOTS)

        @pl.when(jnp.logical_and(jnp.logical_not(active), piece < PIECES))
        def _():
            turn_piece(piece, arena)


def forward(moment, stream, given, arena, saved):
    given = [given] if moment else []
    low, high = saved
    old = ([low] if moment <= SPLIT else []) + ([high] if high is not None else [])
    count = 1 + len(given)
    new = int(moment == SPLIT and high is None)
    output, arena, *kept = pl.pallas_call(
        functools.partial(forward_kernel, moment, stream, len(old)),
        out_shape=[
            pltpu.VMEM((ROWS, D), jnp.bfloat16),
            jax.ShapeDtypeStruct(arena.shape, arena.dtype),
        ]
        + [pltpu.HBM((SPAN, D), jnp.bfloat16)] * (len(old) + new),
        in_specs=[VM] * count + [ANY] * len(old),
        out_specs=[VM, VM] + [ANY] * (len(old) + new),
        input_output_aliases={count - 1 + i: 1 + i for i in range(1 + len(old))},
        scratch_shapes=[pltpu.VMEM((ROWS, D), jnp.bfloat16), pltpu.SemaphoreType.DMA],
        name=f"forward_{moment}_{stream}",
        cost_estimate=cost(moment),
        compiler_params=params(6),
    )(*given, pin(arena), *[far(a) for a in old])
    if moment <= SPLIT:
        low = kept.pop(0)
    return output, arena, (low, kept[0] if kept else None)


def backward_kernel(moment, stream, held, pack, *refs):
    given_ref = refs[0] if moment > LAST else None
    output, arena = refs[len(refs) - held - pack - 2 : len(refs) - held - pack]
    section = lax.axis_index("chain")
    place = moment - TURN + section
    slot = stream * SLOTS + place

    def upstream(part):
        start = ENDS + (stream * SLOTS + moment - LAST) * ROWS
        if moment == LAST:
            given = arena[start : start + ROWS, part]
        elif moment - LAST < SLOTS:
            given = jnp.where(section == LAST, arena[start : start + ROWS, part], given_ref[:, part])
        else:
            given = given_ref[:, part]
        return given.astype(jnp.float32)

    @pl.when(jnp.logical_and(place >= 0, place < SLOTS))
    def _():
        def gelu_part(index, total):
            part = pl.ds(pl.multiple_of(index * COLS, COLS), COLS)
            high = arena[at_slot(HIGH, slot), part].astype(jnp.float32)
            hidden = high + arena[at_slot(LOW, slot), part].astype(jnp.float32)
            _, pullback = jax.vjp(jax.nn.gelu, hidden)
            grad_hidden = pullback(upstream(part))[0].astype(jnp.bfloat16)
            arena[at_slot(GRAD, slot), part] = grad_hidden
            return total + jnp.sum(grad_hidden.astype(jnp.float32) * hidden, axis=-1, keepdims=True)

        total = lax.fori_loop(0, D // COLS, gelu_part, jnp.zeros((ROWS, 1), jnp.float32))
        if moment == TURN + SLOTS - 1:
            return

        @pl.when(section > 0)
        def _():
            inv_rms = inverse_rms(arena[at_slot(INPUT, slot)].astype(jnp.float32))
            mean = total * (1.0 / D)

            def column_part(index, part):
                grad_normed = gain_of(arena, part) * jnp.dot(
                    arena[at_slot(GRAD, slot)],
                    arena[TURNED : TURNED + D, part],
                    preferred_element_type=jnp.float32,
                )
                normed = arena[at_slot(INPUT, slot), part].astype(jnp.float32) * inv_rms
                grad_input = upstream(part) + inv_rms * (grad_normed - normed * mean)
                output[:, part] = grad_input.astype(jnp.bfloat16)

            each_part(column_part)

    if pack:
        packed = refs[-1]
        for chip in range(CHIPS):
            packed[chip] = arena[GRAD : GRAD + SPAN, chip * WIDE : (chip + 1) * WIDE].T


def backward(moment, stream, given, arena, held, pack):
    given = [given] if moment > LAST else []
    count = len(given)
    return pl.pallas_call(
        functools.partial(backward_kernel, moment, stream, len(held), int(pack)),
        out_shape=[
            jax.ShapeDtypeStruct((ROWS, D), jnp.bfloat16),
            jax.ShapeDtypeStruct(arena.shape, arena.dtype),
        ]
        + [pltpu.HBM(a.shape, a.dtype) for a in held]
        + [jax.ShapeDtypeStruct((CHIPS, WIDE, SPAN), jnp.bfloat16)] * pack,
        in_specs=[VM] * (1 + count) + [ANY] * len(held),
        out_specs=[VM, VM] + [ANY] * len(held) + [VM] * pack,
        input_output_aliases={count + i: 1 + i for i in range(1 + len(held))},
        name=f"backward_{moment}_{stream}",
        cost_estimate=cost(moment),
        compiler_params=params(6),
    )(*given, pin(arena), *[far(a) for a in held])


def product_kernel(grads, *refs):
    pieces, (keep, give, held, turned_grads, total, sems) = refs[: 2 * CHIPS], refs[2 * CHIPS :]
    replica = lax.axis_index("dp")
    z_hi, y, core = replica // 8, (replica // 2) % 4, replica % 2
    low = lax.axis_index("chain") < HALF
    chips = [(z_hi if flip == 0 else 1 - z_hi) * 4 + (y + turn) % 4 for flip, turn in PIECE_FROM]

    def load(index, half, column):
        start = pl.multiple_of(chips[index] * SPAN, SPAN)
        part = pl.ds(column * COLS, COLS)
        return pltpu.make_async_copy(
            pieces[half * CHIPS + index].at[:, part], held.at[pl.ds(start, SPAN), part], sems.at[column]
        )

    for column in range(D // COLS):
        for index in range(CHIPS):
            pl.when(low)(load(index, 0, column).start)
            pl.when(jnp.logical_not(low))(load(index, 1, column).start)
    for chip in range(CHIPS):
        turned_grads[:, chip * SPAN : (chip + 1) * SPAN] = grads[chip]
    for column in range(D // COLS):
        part = slice(column * COLS, (column + 1) * COLS)
        pltpu.make_async_copy(held.at[:, part], held.at[:, part], sems.at[column]).wait()
        total[:, part] = jnp.dot(turned_grads[...], held[:, part], preferred_element_type=jnp.float32)

    def turn(chip, carry):
        turned = total[:, pl.ds(pl.multiple_of(chip * WIDE, WIDE), WIDE)].T
        low_rows, high_rows = turned[:SHARE], turned[SHARE:]
        keep[chip] = jnp.where(core == 0, low_rows, high_rows)
        give[chip] = jnp.where(core == 0, high_rows, low_rows).astype(jnp.bfloat16)
        return carry

    lax.fori_loop(0, CHIPS, turn, 0)


def product(grads, pieces):
    block = (CHIPS, SHARE, WIDE)
    return pl.pallas_call(
        product_kernel,
        out_shape=[jax.ShapeDtypeStruct(block, jnp.float32), jax.ShapeDtypeStruct(block, jnp.bfloat16)],
        in_specs=[VM] + [ANY] * len(pieces),
        out_specs=[VM, VM],
        scratch_shapes=[
            pltpu.VMEM((CHIPS * SPAN, D), jnp.bfloat16),
            pltpu.VMEM((WIDE, CHIPS * SPAN), jnp.bfloat16),
            pltpu.VMEM((WIDE, D), jnp.float32),
            pltpu.SemaphoreType.DMA((D // COLS,)),
        ],
        name="weight_product",
        compiler_params=params(36),
    )(grads, *[far(a) for a in pieces])


def add_kernel(keep, taken, whole):
    whole[...] = (keep[...] + taken[...].astype(jnp.float32)).astype(jnp.bfloat16)


def add(keep, taken):
    return pl.pallas_call(
        add_kernel,
        out_shape=jax.ShapeDtypeStruct(taken.shape, taken.dtype),
        in_specs=[VM, VM],
        out_specs=VM,
        name="add_cores",
        compiler_params=params(24),
    )(keep, taken)


def finish_kernel(blocks, weight, rows_ref, sums_ref, own, sem):
    start = pl.multiple_of(lax.axis_index("dp") * SHARE, SHARE)
    load = pltpu.make_async_copy(weight.at[pl.ds(start, SHARE)], own, sem)
    load.start()
    for chip in range(CHIPS):
        rows_ref[:, chip * WIDE : (chip + 1) * WIDE] = blocks[chip]
    load.wait()
    total = jnp.zeros((SHARE, 1), jnp.float32)
    for chip in range(CHIPS):
        part = slice(chip * WIDE, (chip + 1) * WIDE)
        term = own[:, part].astype(jnp.float32) * blocks[chip].astype(jnp.float32)
        total = total + jnp.sum(term, axis=-1, keepdims=True)
    sums_ref[...] = total


def finish(blocks, weight):
    return pl.pallas_call(
        finish_kernel,
        out_shape=[
            jax.ShapeDtypeStruct((SHARE, D), jnp.bfloat16),
            jax.ShapeDtypeStruct((SHARE, 1), jnp.float32),
        ],
        in_specs=[VM, ANY],
        out_specs=[VM, VM],
        scratch_shapes=[pltpu.VMEM((SHARE, D), jnp.bfloat16), pltpu.SemaphoreType.DMA],
        name="weight_rows",
        compiler_params=params(12),
    )(blocks, far(weight))


PIECE_FROM = ((0, 0), (0, 3), (0, 1), (1, 0), (1, 3), (1, 1), (0, 2), (1, 2))


def along(flip, turn):
    pairs = []
    for replica in range(REPLICAS):
        z_hi, y, core = replica // 8, (replica // 2) % 4, replica % 2
        source = (z_hi ^ flip) * 8 + (y + turn) % 4 * 2 + core
        pairs.append((source, replica))
    return pairs


def bring(array, flip, turn, half):
    pairs = [
        (section * REPLICAS + source, section * REPLICAS + target)
        for section in range(half * HALF, (half + 1) * HALF)
        for source, target in along(flip, turn)
    ]
    return lax.ppermute(array, ("chain", "dp"), pairs)


FIRST = ((0, 3), (0, 1), (1, 0))
THEN = ((0, 2), (1, 3), (1, 1), (1, 2))
GATHER = ({(11, 0): FIRST + THEN}, {(12, 0): FIRST, (15, 0): THEN})


def fetch(pieces, name, half):
    if name not in pieces:
        flip, turn = name
        if turn == 0:
            pieces[name] = bring(fetch(pieces, (0, 0), half), 1, 0, half)
        elif turn == 2:
            way = 1 if flip else 3
            pieces[name] = bring(fetch(pieces, (flip, way), half), 0, way, half)
        else:
            pieces[name] = bring(fetch(pieces, (flip, 0), half), 0, turn, half)
    return pieces[name]


def on_device(tokens, cotangent, weights, gains):
    axes = ("chain", "dp")
    output, arena, low = first(
        weights[0], tokens.reshape(SPAN, D), cotangent.reshape(SPAN, D), gains
    )
    saved = (low, None)
    arriving = [None] * STREAMS
    returning = [None] * STREAMS
    pieces = ({}, {})
    for moment in range(TURN + SLOTS):
        sent = list(arriving)
        for stream in range(STREAMS):
            now = (moment, stream)
            if moment < LAST + SLOTS:
                if moment or stream:
                    output, arena, saved = forward(moment, stream, arriving[stream], arena, saved)
                senders = [s for s in range(LAST) if 0 <= moment // 2 * 2 + 1 - s < SLOTS + 1]
                if moment < LAST + SLOTS - 1:
                    sent[stream] = lax.ppermute(output, axes, route(senders, True))
                if now == (SPLIT, STREAMS - 1):
                    pieces[0][0, 0] = saved[0]
                if now == (LAST + SLOTS - 1, STREAMS - 1):
                    pieces[1][0, 0] = saved[1]
            if moment >= LAST:
                held = [
                    (half, name)
                    for half in range(2)
                    for name in GATHER[half].get(now, ())
                ]
                output, arena, *through = backward(
                    moment, stream, returning[stream], arena,
                    [fetch(pieces[half], name, half) for half, name in held],
                    now == (TURN + SLOTS - 1, STREAMS - 1),
                )
                for (half, name), array in zip(held, through):
                    pieces[half][name] = array
                late = LAST + (moment - LAST) // 2 * 2 + 1
                senders = [s for s in range(1, SECTIONS) if 0 <= late - TURN + s < SLOTS + 1]
                if moment < TURN + SLOTS - 1:
                    returning[stream] = lax.ppermute(output, axes, route(senders, False))
        arriving = sent

    chips = [[replica for replica in range(REPLICAS) if replica % 2 == core] for core in range(2)]
    columns = lax.all_to_all(through[-1], "dp", 0, 0, axis_index_groups=chips)
    keep, give = product(columns, [fetch(pieces[half], name, half) for half in range(2) for name in PIECE_FROM])
    other = [(replica ^ 1, replica) for replica in range(REPLICAS)]
    blocks = add(keep, lax.ppermute(give, "dp", other))
    blocks = lax.all_to_all(blocks, "dp", 0, 0, axis_index_groups=chips)
    weight_rows, sums = finish(blocks, weights[0])
    own_gain = lax.dynamic_slice_in_dim(gains[0], lax.axis_index("dp") * SHARE, SHARE, 0)
    return (weight_rows[None], (sums[:, 0] / own_gain)[None])


def solution(mesh):
    placed = (P(None, "dp", None), P(None, "dp", None), P("chain", None, None), P("chain", None))
    return jax.shard_map(
        on_device,
        mesh=mesh,
        in_specs=placed,
        out_specs=(P("chain", "dp", None), P("chain", "dp")),
        check_vma=False,
    )
```

```python
import functools

import jax
import jax.numpy as jnp
from jax import lax
from jax.experimental import pallas as pl
from jax.experimental.pallas import tpu as pltpu
from jax.sharding import PartitionSpec as P

SECTIONS = 8
LAST = SECTIONS - 1
TURN = 2 * LAST
REPLICAS = 16
D = 3072
SPAN = 256
SHARE = D // REPLICAS
CHIPS = REPLICAS // 2
WIDE = D // CHIPS
STREAMS = 2
SLOTS = 2
ROWS = SPAN // (STREAMS * SLOTS)
COLS = 1024
PIECES = 6
PIECE = D // PIECES
TURNED = D
INPUT = 2 * D
GRAD = INPUT + SPAN
ENDS = GRAD + SPAN
HIGH = ENDS + SPAN
LOW = HIGH + SPAN
GAIN = LOW + SPAN
ARENA = GAIN + 16
HALF = SECTIONS // 2
SPLIT = HALF + SLOTS - 2
WEIGHTS = {4: 5, 5: 5, 6: 5, 7: 0, 8: 0, 9: 0, 10: 0, 11: 0, 12: 5, 13: 5, 14: 5}
VM = pl.BlockSpec(memory_space=pltpu.VMEM)
ANY = pl.BlockSpec(memory_space=pl.ANY)


def cost(moment):
    weight = WEIGHTS.get(moment, 20)
    return pl.CostEstimate(flops=weight * 2 * ROWS * D * D, bytes_accessed=4 * D * D, transcendentals=0)


def pin(array):
    return pltpu.with_memory_space_constraint(array, pltpu.VMEM)


def far(array):
    return pltpu.with_memory_space_constraint(array, pltpu.HBM)


def params(mib):
    return pltpu.CompilerParams(vmem_limit_bytes=mib << 20)


def partner(section, replica):
    z_hi, rest = divmod(replica, 8)
    core = rest % 2
    if section % 2 == 0 and core == 1:
        z_hi = 1 - z_hi
    return z_hi * 8 + rest


def route(sections, forward):
    pairs = []
    for section in sections:
        low = section if forward else section - 1
        for replica in range(REPLICAS):
            here, there = low * REPLICAS + replica, (low + 1) * REPLICAS + partner(low, replica)
            pairs.append((here, there) if forward else (there, here))
    return pairs


def inverse_rms(x_float):
    return lax.rsqrt(jnp.mean(x_float * x_float, axis=-1, keepdims=True) + 1e-06)


def at_slot(base, slot):
    return pl.ds(pl.multiple_of(base + slot * ROWS, ROWS), ROWS)


def gain_of(arena, part):
    three = arena[GAIN : GAIN + 16, part].astype(jnp.float32)
    return three[0:1] + three[1:2] + three[2:3]


def each_part(body):
    def run(index, carry):
        body(index, pl.ds(pl.multiple_of(index * COLS, COLS), COLS))
        return carry

    lax.fori_loop(0, D // COLS, run, 0)


def forward_block(slot, given, arena, saved, output, scaled, sem, ready=None):
    arena[at_slot(INPUT, slot)] = given
    x_float = given.astype(jnp.float32)
    scaled[...] = (x_float * inverse_rms(x_float) * gain_of(arena, slice(None))).astype(jnp.bfloat16)
    saves = [pltpu.make_async_copy(scaled, a.at[at_slot(0, slot)], sem) for a in saved]
    if len(saves) == 1:
        saves[0].start()
    else:
        low = lax.axis_index("chain") < HALF
        pl.when(low)(saves[0].start)
        pl.when(jnp.logical_not(low))(saves[1].start)

    def column_part(index, part):
        if ready is not None:
            ready(index)
        hidden = jnp.dot(scaled[...], arena[0:D, part], preferred_element_type=jnp.float32)
        high = hidden.astype(jnp.bfloat16)
        arena[at_slot(HIGH, slot), part] = high
        arena[at_slot(LOW, slot), part] = (hidden - high.astype(jnp.float32)).astype(jnp.bfloat16)
        x_part = arena[at_slot(INPUT, slot), part].astype(jnp.float32)
        output[:, part] = (x_part + jax.nn.gelu(hidden)).astype(jnp.bfloat16)

    each_part(column_part)
    saves[0].wait()


def first_kernel(weight, tokens, cotangent, gain, output, arena, saved, scaled, made, gain_row, sem, loads):
    section = lax.axis_index("chain")
    ends = arena.at[pl.ds(ENDS, SPAN)]
    load_gain = pltpu.make_async_copy(gain, gain_row, loads.at[0])
    load_tokens = pltpu.make_async_copy(tokens, ends, loads.at[1])
    load_cotangent = pltpu.make_async_copy(cotangent, ends, loads.at[1])

    def load_part(index):
        part = pl.ds(pl.multiple_of(index * COLS, COLS), COLS)
        return pltpu.make_async_copy(weight.at[:, part], arena.at[pl.ds(0, D), part], loads.at[2 + index])

    load_gain.start()

    @pl.when(section == 0)
    def _():
        load_tokens.start()

    for index in range(D // COLS):
        load_part(index).start()

    @pl.when(section == LAST)
    def _():
        load_cotangent.start()

    load_gain.wait()
    row = gain_row[...]
    high = row.astype(jnp.bfloat16).astype(jnp.float32)
    middle = (row - high).astype(jnp.bfloat16).astype(jnp.float32)
    blank = jnp.zeros((13, D), jnp.float32)
    three = jnp.concatenate([high, middle, row - high - middle, blank], axis=0)
    arena[GAIN : GAIN + 16] = three.astype(jnp.bfloat16)

    @pl.when(section == 0)
    def _():
        load_tokens.wait()
        given = arena[ENDS : ENDS + ROWS]
        forward_block(0, given, arena, [saved], made, scaled, sem, lambda index: load_part(index).wait())
        pltpu.sync_copy(made, output)

    @pl.when(section != 0)
    def _():
        for index in range(D // COLS):
            load_part(index).wait()

    @pl.when(section == LAST)
    def _():
        load_cotangent.wait()


def first(weight, tokens, cotangent, gain):
    return pl.pallas_call(
        first_kernel,
        out_shape=[
            pltpu.HBM((ROWS, D), jnp.bfloat16),
            pltpu.VMEM((ARENA, D), jnp.bfloat16),
            pltpu.HBM((SPAN, D), jnp.bfloat16),
        ],
        in_specs=[ANY] * 4,
        out_specs=[ANY, VM, ANY],
        scratch_shapes=[
            pltpu.VMEM((ROWS, D), jnp.bfloat16),
            pltpu.VMEM((ROWS, D), jnp.bfloat16),
            pltpu.VMEM((1, D), jnp.float32),
            pltpu.SemaphoreType.DMA,
            pltpu.SemaphoreType.DMA((2 + D // COLS,)),
        ],
        name="load_and_first_block",
        cost_estimate=cost(0),
        compiler_params=params(6),
    )(far(weight), far(tokens), far(cotangent), far(gain))


def turn_piece(piece, arena):
    step = 256

    def run(index, carry):
        start = pl.multiple_of(piece * PIECE + index * step, step)
        arena[TURNED : TURNED + D, pl.ds(start, step)] = arena[pl.ds(start, step), :].T
        return carry

    lax.fori_loop(0, PIECE // step, run, 0)


def forward_kernel(moment, stream, old, *refs):
    given_ref = refs[0] if moment else None
    output, arena, *saves, scaled, sem = refs[int(moment > 0) + 1 + old :]
    section = lax.axis_index("chain")
    place = moment - section
    active = jnp.logical_and(place >= 0, place < SLOTS)

    @pl.when(active)
    def _():
        start = ENDS + (stream * SLOTS + moment) * ROWS
        if moment == 0:
            given = arena[start : start + ROWS]
        elif moment < SLOTS:
            given = jnp.where(section == 0, arena[start : start + ROWS], given_ref[...])
        else:
            given = given_ref[...]
        forward_block(stream * SLOTS + place, given, arena, saves, output, scaled, sem)

    if stream == STREAMS - 1 and moment < PIECES + SLOTS:
        piece = jnp.where(place < 0, moment, moment - SLOTS)

        @pl.when(jnp.logical_and(jnp.logical_not(active), piece < PIECES))
        def _():
            turn_piece(piece, arena)


def forward(moment, stream, given, arena, saved):
    given = [given] if moment else []
    low, high = saved
    old = ([low] if moment <= SPLIT else []) + ([high] if high is not None else [])
    count = 1 + len(given)
    new = int(moment == SPLIT and high is None)
    output, arena, *kept = pl.pallas_call(
        functools.partial(forward_kernel, moment, stream, len(old)),
        out_shape=[
            pltpu.VMEM((ROWS, D), jnp.bfloat16),
            jax.ShapeDtypeStruct(arena.shape, arena.dtype),
        ]
        + [pltpu.HBM((SPAN, D), jnp.bfloat16)] * (len(old) + new),
        in_specs=[VM] * count + [ANY] * len(old),
        out_specs=[VM, VM] + [ANY] * (len(old) + new),
        input_output_aliases={count - 1 + i: 1 + i for i in range(1 + len(old))},
        scratch_shapes=[pltpu.VMEM((ROWS, D), jnp.bfloat16), pltpu.SemaphoreType.DMA],
        name=f"forward_{moment}_{stream}",
        cost_estimate=cost(moment),
        compiler_params=params(6),
    )(*given, pin(arena), *[far(a) for a in old])
    if moment <= SPLIT:
        low = kept.pop(0)
    return output, arena, (low, kept[0] if kept else None)


def backward_kernel(moment, stream, held, pack, *refs):
    given_ref = refs[0] if moment > LAST else None
    output, arena = refs[len(refs) - held - pack - 2 : len(refs) - held - pack]
    section = lax.axis_index("chain")
    place = moment - TURN + section
    slot = stream * SLOTS + place

    def upstream(part):
        start = ENDS + (stream * SLOTS + moment - LAST) * ROWS
        if moment == LAST:
            given = arena[start : start + ROWS, part]
        elif moment - LAST < SLOTS:
            given = jnp.where(section == LAST, arena[start : start + ROWS, part], given_ref[:, part])
        else:
            given = given_ref[:, part]
        return given.astype(jnp.float32)

    @pl.when(jnp.logical_and(place >= 0, place < SLOTS))
    def _():
        def gelu_part(index, total):
            part = pl.ds(pl.multiple_of(index * COLS, COLS), COLS)
            high = arena[at_slot(HIGH, slot), part].astype(jnp.float32)
            hidden = high + arena[at_slot(LOW, slot), part].astype(jnp.float32)
            _, pullback = jax.vjp(jax.nn.gelu, hidden)
            grad_hidden = pullback(upstream(part))[0].astype(jnp.bfloat16)
            arena[at_slot(GRAD, slot), part] = grad_hidden
            return total + jnp.sum(grad_hidden.astype(jnp.float32) * hidden, axis=-1, keepdims=True)

        total = lax.fori_loop(0, D // COLS, gelu_part, jnp.zeros((ROWS, 1), jnp.float32))
        if moment == TURN + SLOTS - 1:
            return

        @pl.when(section > 0)
        def _():
            inv_rms = inverse_rms(arena[at_slot(INPUT, slot)].astype(jnp.float32))
            mean = total * (1.0 / D)

            def column_part(index, part):
                grad_normed = gain_of(arena, part) * jnp.dot(
                    arena[at_slot(GRAD, slot)],
                    arena[TURNED : TURNED + D, part],
                    preferred_element_type=jnp.float32,
                )
                normed = arena[at_slot(INPUT, slot), part].astype(jnp.float32) * inv_rms
                grad_input = upstream(part) + inv_rms * (grad_normed - normed * mean)
                output[:, part] = grad_input.astype(jnp.bfloat16)

            each_part(column_part)

    if pack:
        packed = refs[-1]
        for chip in range(CHIPS):
            packed[chip] = arena[GRAD : GRAD + SPAN, chip * WIDE : (chip + 1) * WIDE].T


def backward(moment, stream, given, arena, held, pack):
    given = [given] if moment > LAST else []
    count = len(given)
    return pl.pallas_call(
        functools.partial(backward_kernel, moment, stream, len(held), int(pack)),
        out_shape=[
            jax.ShapeDtypeStruct((ROWS, D), jnp.bfloat16),
            jax.ShapeDtypeStruct(arena.shape, arena.dtype),
        ]
        + [pltpu.HBM(a.shape, a.dtype) for a in held]
        + [jax.ShapeDtypeStruct((CHIPS, WIDE, SPAN), jnp.bfloat16)] * pack,
        in_specs=[VM] * (1 + count) + [ANY] * len(held),
        out_specs=[VM, VM] + [ANY] * len(held) + [VM] * pack,
        input_output_aliases={count + i: 1 + i for i in range(1 + len(held))},
        name=f"backward_{moment}_{stream}",
        cost_estimate=cost(moment),
        compiler_params=params(6),
    )(*given, pin(arena), *[far(a) for a in held])


def product_kernel(grads, *refs):
    pieces, (keep, give, held, turned_grads, total, sems) = refs[: 2 * CHIPS], refs[2 * CHIPS :]
    replica = lax.axis_index("dp")
    z_hi, y, core = replica // 8, (replica // 2) % 4, replica % 2
    low = lax.axis_index("chain") < HALF
    chips = [(z_hi if flip == 0 else 1 - z_hi) * 4 + (y + turn) % 4 for flip, turn in PIECE_FROM]

    def load(index, half, column):
        start = pl.multiple_of(chips[index] * SPAN, SPAN)
        part = pl.ds(column * COLS, COLS)
        return pltpu.make_async_copy(
            pieces[half * CHIPS + index].at[:, part], held.at[pl.ds(start, SPAN), part], sems.at[column]
        )

    for column in range(D // COLS):
        for index in range(CHIPS):
            pl.when(low)(load(index, 0, column).start)
            pl.when(jnp.logical_not(low))(load(index, 1, column).start)
    for chip in range(CHIPS):
        turned_grads[:, chip * SPAN : (chip + 1) * SPAN] = grads[chip]
    for column in range(D // COLS):
        part = slice(column * COLS, (column + 1) * COLS)
        pltpu.make_async_copy(held.at[:, part], held.at[:, part], sems.at[column]).wait()
        total[:, part] = jnp.dot(turned_grads[...], held[:, part], preferred_element_type=jnp.float32)

    def turn(chip, carry):
        turned = total[:, pl.ds(pl.multiple_of(chip * WIDE, WIDE), WIDE)].T
        low_rows, high_rows = turned[:SHARE], turned[SHARE:]
        keep[chip] = jnp.where(core == 0, low_rows, high_rows)
        give[chip] = jnp.where(core == 0, high_rows, low_rows).astype(jnp.bfloat16)
        return carry

    lax.fori_loop(0, CHIPS, turn, 0)


def product(grads, pieces):
    block = (CHIPS, SHARE, WIDE)
    return pl.pallas_call(
        product_kernel,
        out_shape=[jax.ShapeDtypeStruct(block, jnp.float32), jax.ShapeDtypeStruct(block, jnp.bfloat16)],
        in_specs=[VM] + [ANY] * len(pieces),
        out_specs=[VM, VM],
        scratch_shapes=[
            pltpu.VMEM((CHIPS * SPAN, D), jnp.bfloat16),
            pltpu.VMEM((WIDE, CHIPS * SPAN), jnp.bfloat16),
            pltpu.VMEM((WIDE, D), jnp.float32),
            pltpu.SemaphoreType.DMA((D // COLS,)),
        ],
        name="weight_product",
        compiler_params=params(36),
    )(grads, *[far(a) for a in pieces])


def add_kernel(keep, taken, whole):
    whole[...] = (keep[...] + taken[...].astype(jnp.float32)).astype(jnp.bfloat16)


def add(keep, taken):
    return pl.pallas_call(
        add_kernel,
        out_shape=jax.ShapeDtypeStruct(taken.shape, taken.dtype),
        in_specs=[VM, VM],
        out_specs=VM,
        name="add_cores",
        compiler_params=params(24),
    )(keep, taken)


def finish_kernel(blocks, weight, rows_ref, sums_ref, own, sem):
    start = pl.multiple_of(lax.axis_index("dp") * SHARE, SHARE)
    load = pltpu.make_async_copy(weight.at[pl.ds(start, SHARE)], own, sem)
    load.start()
    for chip in range(CHIPS):
        rows_ref[:, chip * WIDE : (chip + 1) * WIDE] = blocks[chip]
    load.wait()
    total = jnp.zeros((SHARE, 1), jnp.float32)
    for chip in range(CHIPS):
        part = slice(chip * WIDE, (chip + 1) * WIDE)
        term = own[:, part].astype(jnp.float32) * blocks[chip].astype(jnp.float32)
        total = total + jnp.sum(term, axis=-1, keepdims=True)
    sums_ref[...] = total


def finish(blocks, weight):
    return pl.pallas_call(
        finish_kernel,
        out_shape=[
            jax.ShapeDtypeStruct((SHARE, D), jnp.bfloat16),
            jax.ShapeDtypeStruct((SHARE, 1), jnp.float32),
        ],
        in_specs=[VM, ANY],
        out_specs=[VM, VM],
        scratch_shapes=[pltpu.VMEM((SHARE, D), jnp.bfloat16), pltpu.SemaphoreType.DMA],
        name="weight_rows",
        compiler_params=params(12),
    )(blocks, far(weight))


PIECE_FROM = ((0, 0), (0, 3), (0, 1), (1, 0), (1, 3), (1, 1), (0, 2), (1, 2))


def along(flip, turn):
    pairs = []
    for replica in range(REPLICAS):
        z_hi, y, core = replica // 8, (replica // 2) % 4, replica % 2
        source = (z_hi ^ flip) * 8 + (y + turn) % 4 * 2 + core
        pairs.append((source, replica))
    return pairs


def bring(array, flip, turn, half):
    pairs = [
        (section * REPLICAS + source, section * REPLICAS + target)
        for section in range(half * HALF, (half + 1) * HALF)
        for source, target in along(flip, turn)
    ]
    return lax.ppermute(array, ("chain", "dp"), pairs)


FIRST = ((0, 3), (0, 1), (1, 0))
THEN = ((0, 2), (1, 3), (1, 1), (1, 2))
GATHER = ({(7, 0): FIRST, (10, 1): THEN[:3], (14, 0): THEN[3:]}, {(12, 1): FIRST, (15, 1): THEN[:3]})


def fetch(pieces, name, half):
    if name not in pieces:
        flip, turn = name
        if turn == 0:
            pieces[name] = bring(fetch(pieces, (0, 0), half), 1, 0, half)
        elif turn == 2:
            way = 1 if flip else 3
            pieces[name] = bring(fetch(pieces, (flip, way), half), 0, way, half)
        else:
            pieces[name] = bring(fetch(pieces, (flip, 0), half), 0, turn, half)
    return pieces[name]


def on_device(tokens, cotangent, weights, gains):
    axes = ("chain", "dp")
    output, arena, low = first(
        weights[0], tokens.reshape(SPAN, D), cotangent.reshape(SPAN, D), gains
    )
    saved = (low, None)
    arriving = [None] * STREAMS
    returning = [None] * STREAMS
    pieces = ({}, {})
    for moment in range(TURN + SLOTS):
        sent = list(arriving)
        for stream in range(STREAMS):
            now = (moment, stream)
            if moment < LAST + SLOTS:
                if moment or stream:
                    output, arena, saved = forward(moment, stream, arriving[stream], arena, saved)
                senders = [s for s in range(LAST) if 0 <= moment // 2 * 2 + 1 - s < SLOTS + 1]
                if moment < LAST + SLOTS - 1:
                    sent[stream] = lax.ppermute(output, axes, route(senders, True))
                if now == (SPLIT, STREAMS - 1):
                    pieces[0][0, 0] = saved[0]
                if now == (LAST + SLOTS - 1, STREAMS - 1):
                    pieces[1][0, 0] = saved[1]
            if moment >= LAST:
                held = [
                    (half, name)
                    for half in range(2)
                    for name in GATHER[half].get(now, ())
                ]
                output, arena, *through = backward(
                    moment, stream, returning[stream], arena,
                    [fetch(pieces[half], name, half) for half, name in held],
                    now == (TURN + SLOTS - 1, STREAMS - 1),
                )
                for (half, name), array in zip(held, through):
                    pieces[half][name] = array
                late = LAST + (moment - LAST) // 2 * 2 + 1
                senders = [s for s in range(1, SECTIONS) if 0 <= late - TURN + s < SLOTS + 1]
                if moment < TURN + SLOTS - 1:
                    returning[stream] = lax.ppermute(output, axes, route(senders, False))
        arriving = sent

    chips = [[replica for replica in range(REPLICAS) if replica % 2 == core] for core in range(2)]
    columns = lax.all_to_all(through[-1], "dp", 0, 0, axis_index_groups=chips)
    keep, give = product(columns, [fetch(pieces[half], name, half) for half in range(2) for name in PIECE_FROM])
    other = [(replica ^ 1, replica) for replica in range(REPLICAS)]
    blocks = add(keep, lax.ppermute(give, "dp", other))
    blocks = lax.all_to_all(blocks, "dp", 0, 0, axis_index_groups=chips)
    weight_rows, sums = finish(blocks, weights[0])
    own_gain = lax.dynamic_slice_in_dim(gains[0], lax.axis_index("dp") * SHARE, SHARE, 0)
    return (weight_rows[None], (sums[:, 0] / own_gain)[None])


def solution(mesh):
    placed = (P(None, "dp", None), P(None, "dp", None), P("chain", None, None), P("chain", None))
    return jax.shard_map(
        on_device,
        mesh=mesh,
        in_specs=placed,
        out_specs=(P("chain", "dp", None), P("chain", "dp")),
        check_vma=False,
    )
```

```python
import functools

import jax
import jax.numpy as jnp
from jax import lax
from jax.experimental import pallas as pl
from jax.experimental.pallas import tpu as pltpu
from jax.sharding import PartitionSpec as P

SECTIONS = 8
LAST = SECTIONS - 1
TURN = 2 * LAST
REPLICAS = 16
D = 3072
SPAN = 256
SHARE = D // REPLICAS
CHIPS = REPLICAS // 2
WIDE = D // CHIPS
STREAMS = 2
SLOTS = 2
ROWS = SPAN // (STREAMS * SLOTS)
COLS = 1024
PIECES = 6
PIECE = D // PIECES
TURNED = D
INPUT = 2 * D
GRAD = INPUT + SPAN
ENDS = GRAD + SPAN
HIGH = ENDS + SPAN
LOW = HIGH + SPAN
GAIN = LOW + SPAN
ARENA = GAIN + 16
HALF = SECTIONS // 2
SPLIT = HALF + SLOTS - 2
WEIGHTS = {4: 5, 5: 5, 6: 5, 7: 0, 8: 0, 9: 0, 10: 0, 11: 0, 12: 5, 13: 5, 14: 5}
VM = pl.BlockSpec(memory_space=pltpu.VMEM)
ANY = pl.BlockSpec(memory_space=pl.ANY)


def cost(moment):
    weight = WEIGHTS.get(moment, 20)
    return pl.CostEstimate(flops=weight * 2 * ROWS * D * D, bytes_accessed=4 * D * D, transcendentals=0)


def pin(array):
    return pltpu.with_memory_space_constraint(array, pltpu.VMEM)


def far(array):
    return pltpu.with_memory_space_constraint(array, pltpu.HBM)


def params(mib):
    return pltpu.CompilerParams(vmem_limit_bytes=mib << 20)


def partner(section, replica):
    z_hi, rest = divmod(replica, 8)
    core = rest % 2
    if section % 2 == 0 and core == 1:
        z_hi = 1 - z_hi
    return z_hi * 8 + rest


def route(sections, forward):
    pairs = []
    for section in sections:
        low = section if forward else section - 1
        for replica in range(REPLICAS):
            here, there = low * REPLICAS + replica, (low + 1) * REPLICAS + partner(low, replica)
            pairs.append((here, there) if forward else (there, here))
    return pairs


def inverse_rms(x_float):
    return lax.rsqrt(jnp.mean(x_float * x_float, axis=-1, keepdims=True) + 1e-06)


def at_slot(base, slot):
    return pl.ds(pl.multiple_of(base + slot * ROWS, ROWS), ROWS)


def gain_of(arena, part):
    three = arena[GAIN : GAIN + 16, part].astype(jnp.float32)
    return three[0:1] + three[1:2] + three[2:3]


def each_part(body):
    def run(index, carry):
        body(index, pl.ds(pl.multiple_of(index * COLS, COLS), COLS))
        return carry

    lax.fori_loop(0, D // COLS, run, 0)


def forward_block(slot, given, arena, saved, output, scaled, sem, ready=None):
    arena[at_slot(INPUT, slot)] = given
    x_float = given.astype(jnp.float32)
    scaled[...] = (x_float * inverse_rms(x_float) * gain_of(arena, slice(None))).astype(jnp.bfloat16)
    saves = [pltpu.make_async_copy(scaled, a.at[at_slot(0, slot)], sem) for a in saved]
    if len(saves) == 1:
        saves[0].start()
    else:
        low = lax.axis_index("chain") < HALF
        pl.when(low)(saves[0].start)
        pl.when(jnp.logical_not(low))(saves[1].start)

    def column_part(index, part):
        if ready is not None:
            ready(index)
        hidden = jnp.dot(scaled[...], arena[0:D, part], preferred_element_type=jnp.float32)
        high = hidden.astype(jnp.bfloat16)
        arena[at_slot(HIGH, slot), part] = high
        arena[at_slot(LOW, slot), part] = (hidden - high.astype(jnp.float32)).astype(jnp.bfloat16)
        x_part = arena[at_slot(INPUT, slot), part].astype(jnp.float32)
        output[:, part] = (x_part + jax.nn.gelu(hidden)).astype(jnp.bfloat16)

    each_part(column_part)
    saves[0].wait()


def first_kernel(weight, tokens, cotangent, gain, output, arena, saved, scaled, made, gain_row, sem, loads):
    section = lax.axis_index("chain")
    ends = arena.at[pl.ds(ENDS, SPAN)]
    load_gain = pltpu.make_async_copy(gain, gain_row, loads.at[0])
    load_tokens = pltpu.make_async_copy(tokens, ends, loads.at[1])
    load_cotangent = pltpu.make_async_copy(cotangent, ends, loads.at[1])

    def load_part(index):
        part = pl.ds(pl.multiple_of(index * COLS, COLS), COLS)
        return pltpu.make_async_copy(weight.at[:, part], arena.at[pl.ds(0, D), part], loads.at[2 + index])

    load_gain.start()

    @pl.when(section == 0)
    def _():
        load_tokens.start()

    for index in range(D // COLS):
        load_part(index).start()

    @pl.when(section == LAST)
    def _():
        load_cotangent.start()

    load_gain.wait()
    row = gain_row[...]
    high = row.astype(jnp.bfloat16).astype(jnp.float32)
    middle = (row - high).astype(jnp.bfloat16).astype(jnp.float32)
    blank = jnp.zeros((13, D), jnp.float32)
    three = jnp.concatenate([high, middle, row - high - middle, blank], axis=0)
    arena[GAIN : GAIN + 16] = three.astype(jnp.bfloat16)

    @pl.when(section == 0)
    def _():
        load_tokens.wait()
        given = arena[ENDS : ENDS + ROWS]
        forward_block(0, given, arena, [saved], made, scaled, sem, lambda index: load_part(index).wait())
        pltpu.sync_copy(made, output)

    @pl.when(section != 0)
    def _():
        for index in range(D // COLS):
            load_part(index).wait()

    @pl.when(section == LAST)
    def _():
        load_cotangent.wait()


def first(weight, tokens, cotangent, gain):
    return pl.pallas_call(
        first_kernel,
        out_shape=[
            pltpu.HBM((ROWS, D), jnp.bfloat16),
            pltpu.VMEM((ARENA, D), jnp.bfloat16),
            pltpu.HBM((SPAN, D), jnp.bfloat16),
        ],
        in_specs=[ANY] * 4,
        out_specs=[ANY, VM, ANY],
        scratch_shapes=[
            pltpu.VMEM((ROWS, D), jnp.bfloat16),
            pltpu.VMEM((ROWS, D), jnp.bfloat16),
            pltpu.VMEM((1, D), jnp.float32),
            pltpu.SemaphoreType.DMA,
            pltpu.SemaphoreType.DMA((2 + D // COLS,)),
        ],
        name="load_and_first_block",
        cost_estimate=cost(0),
        compiler_params=params(6),
    )(far(weight), far(tokens), far(cotangent), far(gain))


def turn_piece(piece, arena):
    step = 256

    def run(index, carry):
        start = pl.multiple_of(piece * PIECE + index * step, step)
        arena[TURNED : TURNED + D, pl.ds(start, step)] = arena[pl.ds(start, step), :].T
        return carry

    lax.fori_loop(0, PIECE // step, run, 0)


def forward_kernel(moment, stream, old, *refs):
    given_ref = refs[0] if moment else None
    output, arena, *saves, scaled, sem = refs[int(moment > 0) + 1 + old :]
    section = lax.axis_index("chain")
    place = moment - section
    active = jnp.logical_and(place >= 0, place < SLOTS)

    @pl.when(active)
    def _():
        start = ENDS + (stream * SLOTS + moment) * ROWS
        if moment == 0:
            given = arena[start : start + ROWS]
        elif moment < SLOTS:
            given = jnp.where(section == 0, arena[start : start + ROWS], given_ref[...])
        else:
            given = given_ref[...]
        forward_block(stream * SLOTS + place, given, arena, saves, output, scaled, sem)

    if stream == STREAMS - 1 and moment < PIECES + SLOTS:
        piece = jnp.where(place < 0, moment, moment - SLOTS)

        @pl.when(jnp.logical_and(jnp.logical_not(active), piece < PIECES))
        def _():
            turn_piece(piece, arena)


def forward(moment, stream, given, arena, saved):
    given = [given] if moment else []
    low, high = saved
    old = ([low] if moment <= SPLIT else []) + ([high] if high is not None else [])
    count = 1 + len(given)
    new = int(moment == SPLIT and high is None)
    output, arena, *kept = pl.pallas_call(
        functools.partial(forward_kernel, moment, stream, len(old)),
        out_shape=[
            pltpu.VMEM((ROWS, D), jnp.bfloat16),
            jax.ShapeDtypeStruct(arena.shape, arena.dtype),
        ]
        + [pltpu.HBM((SPAN, D), jnp.bfloat16)] * (len(old) + new),
        in_specs=[VM] * count + [ANY] * len(old),
        out_specs=[VM, VM] + [ANY] * (len(old) + new),
        input_output_aliases={count - 1 + i: 1 + i for i in range(1 + len(old))},
        scratch_shapes=[pltpu.VMEM((ROWS, D), jnp.bfloat16), pltpu.SemaphoreType.DMA],
        name=f"forward_{moment}_{stream}",
        cost_estimate=cost(moment),
        compiler_params=params(6),
    )(*given, pin(arena), *[far(a) for a in old])
    if moment <= SPLIT:
        low = kept.pop(0)
    return output, arena, (low, kept[0] if kept else None)


def backward_kernel(moment, stream, held, pack, *refs):
    given_ref = refs[0] if moment > LAST else None
    output, arena = refs[len(refs) - held - pack - 2 : len(refs) - held - pack]
    section = lax.axis_index("chain")
    place = moment - TURN + section
    slot = stream * SLOTS + place

    def upstream(part):
        start = ENDS + (stream * SLOTS + moment - LAST) * ROWS
        if moment == LAST:
            given = arena[start : start + ROWS, part]
        elif moment - LAST < SLOTS:
            given = jnp.where(section == LAST, arena[start : start + ROWS, part], given_ref[:, part])
        else:
            given = given_ref[:, part]
        return given.astype(jnp.float32)

    @pl.when(jnp.logical_and(place >= 0, place < SLOTS))
    def _():
        def gelu_part(index, total):
            part = pl.ds(pl.multiple_of(index * COLS, COLS), COLS)
            high = arena[at_slot(HIGH, slot), part].astype(jnp.float32)
            hidden = high + arena[at_slot(LOW, slot), part].astype(jnp.float32)
            _, pullback = jax.vjp(jax.nn.gelu, hidden)
            grad_hidden = pullback(upstream(part))[0].astype(jnp.bfloat16)
            arena[at_slot(GRAD, slot), part] = grad_hidden
            return total + jnp.sum(grad_hidden.astype(jnp.float32) * hidden, axis=-1, keepdims=True)

        total = lax.fori_loop(0, D // COLS, gelu_part, jnp.zeros((ROWS, 1), jnp.float32))
        if moment == TURN + SLOTS - 1:
            return

        @pl.when(section > 0)
        def _():
            inv_rms = inverse_rms(arena[at_slot(INPUT, slot)].astype(jnp.float32))
            mean = total * (1.0 / D)

            def column_part(index, part):
                grad_normed = gain_of(arena, part) * jnp.dot(
                    arena[at_slot(GRAD, slot)],
                    arena[TURNED : TURNED + D, part],
                    preferred_element_type=jnp.float32,
                )
                normed = arena[at_slot(INPUT, slot), part].astype(jnp.float32) * inv_rms
                grad_input = upstream(part) + inv_rms * (grad_normed - normed * mean)
                output[:, part] = grad_input.astype(jnp.bfloat16)

            each_part(column_part)

    if pack:
        packed = refs[-1]
        for chip in range(CHIPS):
            packed[chip] = arena[GRAD : GRAD + SPAN, chip * WIDE : (chip + 1) * WIDE].T


def backward(moment, stream, given, arena, held, pack):
    given = [given] if moment > LAST else []
    count = len(given)
    return pl.pallas_call(
        functools.partial(backward_kernel, moment, stream, len(held), int(pack)),
        out_shape=[
            jax.ShapeDtypeStruct((ROWS, D), jnp.bfloat16),
            jax.ShapeDtypeStruct(arena.shape, arena.dtype),
        ]
        + [pltpu.HBM(a.shape, a.dtype) for a in held]
        + [jax.ShapeDtypeStruct((CHIPS, WIDE, SPAN), jnp.bfloat16)] * pack,
        in_specs=[VM] * (1 + count) + [ANY] * len(held),
        out_specs=[VM, VM] + [ANY] * len(held) + [VM] * pack,
        input_output_aliases={count + i: 1 + i for i in range(1 + len(held))},
        name=f"backward_{moment}_{stream}",
        cost_estimate=cost(moment),
        compiler_params=params(6),
    )(*given, pin(arena), *[far(a) for a in held])


def product_kernel(grads, *refs):
    pieces, (keep, give, held, turned_grads, total, sems) = refs[: 2 * CHIPS], refs[2 * CHIPS :]
    replica = lax.axis_index("dp")
    z_hi, y, core = replica // 8, (replica // 2) % 4, replica % 2
    low = lax.axis_index("chain") < HALF
    chips = [(z_hi if flip == 0 else 1 - z_hi) * 4 + (y + turn) % 4 for flip, turn in PIECE_FROM]

    def load(index, half, column):
        start = pl.multiple_of(chips[index] * SPAN, SPAN)
        part = pl.ds(column * COLS, COLS)
        return pltpu.make_async_copy(
            pieces[half * CHIPS + index].at[:, part], held.at[pl.ds(start, SPAN), part], sems.at[column]
        )

    for column in range(D // COLS):
        for index in range(CHIPS):
            pl.when(low)(load(index, 0, column).start)
            pl.when(jnp.logical_not(low))(load(index, 1, column).start)
    for chip in range(CHIPS):
        turned_grads[:, chip * SPAN : (chip + 1) * SPAN] = grads[chip]
    for column in range(D // COLS):
        part = slice(column * COLS, (column + 1) * COLS)
        pltpu.make_async_copy(held.at[:, part], held.at[:, part], sems.at[column]).wait()
        total[:, part] = jnp.dot(turned_grads[...], held[:, part], preferred_element_type=jnp.float32)

    def turn(chip, carry):
        turned = total[:, pl.ds(pl.multiple_of(chip * WIDE, WIDE), WIDE)].T
        low_rows, high_rows = turned[:SHARE], turned[SHARE:]
        keep[chip] = jnp.where(core == 0, low_rows, high_rows)
        give[chip] = jnp.where(core == 0, high_rows, low_rows).astype(jnp.bfloat16)
        return carry

    lax.fori_loop(0, CHIPS, turn, 0)


def product(grads, pieces):
    block = (CHIPS, SHARE, WIDE)
    return pl.pallas_call(
        product_kernel,
        out_shape=[jax.ShapeDtypeStruct(block, jnp.float32), jax.ShapeDtypeStruct(block, jnp.bfloat16)],
        in_specs=[VM] + [ANY] * len(pieces),
        out_specs=[VM, VM],
        scratch_shapes=[
            pltpu.VMEM((CHIPS * SPAN, D), jnp.bfloat16),
            pltpu.VMEM((WIDE, CHIPS * SPAN), jnp.bfloat16),
            pltpu.VMEM((WIDE, D), jnp.float32),
            pltpu.SemaphoreType.DMA((D // COLS,)),
        ],
        name="weight_product",
        compiler_params=params(36),
    )(grads, *[far(a) for a in pieces])


def add_kernel(keep, taken, whole):
    whole[...] = (keep[...] + taken[...].astype(jnp.float32)).astype(jnp.bfloat16)


def add(keep, taken):
    return pl.pallas_call(
        add_kernel,
        out_shape=jax.ShapeDtypeStruct(taken.shape, taken.dtype),
        in_specs=[VM, VM],
        out_specs=VM,
        name="add_cores",
        compiler_params=params(24),
    )(keep, taken)


def finish_kernel(blocks, weight, rows_ref, sums_ref, own, sem):
    start = pl.multiple_of(lax.axis_index("dp") * SHARE, SHARE)
    load = pltpu.make_async_copy(weight.at[pl.ds(start, SHARE)], own, sem)
    load.start()
    for chip in range(CHIPS):
        rows_ref[:, chip * WIDE : (chip + 1) * WIDE] = blocks[chip]
    load.wait()
    total = jnp.zeros((SHARE, 1), jnp.float32)
    for chip in range(CHIPS):
        part = slice(chip * WIDE, (chip + 1) * WIDE)
        term = own[:, part].astype(jnp.float32) * blocks[chip].astype(jnp.float32)
        total = total + jnp.sum(term, axis=-1, keepdims=True)
    sums_ref[...] = total


def finish(blocks, weight):
    return pl.pallas_call(
        finish_kernel,
        out_shape=[
            jax.ShapeDtypeStruct((SHARE, D), jnp.bfloat16),
            jax.ShapeDtypeStruct((SHARE, 1), jnp.float32),
        ],
        in_specs=[VM, ANY],
        out_specs=[VM, VM],
        scratch_shapes=[pltpu.VMEM((SHARE, D), jnp.bfloat16), pltpu.SemaphoreType.DMA],
        name="weight_rows",
        compiler_params=params(12),
    )(blocks, far(weight))


PIECE_FROM = ((0, 0), (0, 3), (0, 1), (1, 0), (1, 3), (1, 1), (0, 2), (1, 2))


def along(flip, turn):
    pairs = []
    for replica in range(REPLICAS):
        z_hi, y, core = replica // 8, (replica // 2) % 4, replica % 2
        source = (z_hi ^ flip) * 8 + (y + turn) % 4 * 2 + core
        pairs.append((source, replica))
    return pairs


def bring(array, flip, turn, half):
    pairs = [
        (section * REPLICAS + source, section * REPLICAS + target)
        for section in range(half * HALF, (half + 1) * HALF)
        for source, target in along(flip, turn)
    ]
    return lax.ppermute(array, ("chain", "dp"), pairs)


FIRST = ((0, 3), (0, 1), (1, 0))
THEN = ((0, 2), (1, 3), (1, 1), (1, 2))
GATHER = ({(7, 0): FIRST, (12, 0): THEN[:3], (15, 0): THEN[3:]}, {(12, 1): FIRST, (15, 1): THEN[:3]})


def fetch(pieces, name, half):
    if name not in pieces:
        flip, turn = name
        if turn == 0:
            pieces[name] = bring(fetch(pieces, (0, 0), half), 1, 0, half)
        elif turn == 2:
            way = 1 if flip else 3
            pieces[name] = bring(fetch(pieces, (flip, way), half), 0, way, half)
        else:
            pieces[name] = bring(fetch(pieces, (flip, 0), half), 0, turn, half)
    return pieces[name]


def on_device(tokens, cotangent, weights, gains):
    axes = ("chain", "dp")
    output, arena, low = first(
        weights[0], tokens.reshape(SPAN, D), cotangent.reshape(SPAN, D), gains
    )
    saved = (low, None)
    arriving = [None] * STREAMS
    returning = [None] * STREAMS
    pieces = ({}, {})
    for moment in range(TURN + SLOTS):
        sent = list(arriving)
        for stream in range(STREAMS):
            now = (moment, stream)
            if moment < LAST + SLOTS:
                if moment or stream:
                    output, arena, saved = forward(moment, stream, arriving[stream], arena, saved)
                senders = [s for s in range(LAST) if 0 <= moment // 2 * 2 + 1 - s < SLOTS + 1]
                if moment < LAST + SLOTS - 1:
                    sent[stream] = lax.ppermute(output, axes, route(senders, True))
                if now == (SPLIT, STREAMS - 1):
                    pieces[0][0, 0] = saved[0]
                if now == (LAST + SLOTS - 1, STREAMS - 1):
                    pieces[1][0, 0] = saved[1]
            if moment >= LAST:
                held = [
                    (half, name)
                    for half in range(2)
                    for name in GATHER[half].get(now, ())
                ]
                output, arena, *through = backward(
                    moment, stream, returning[stream], arena,
                    [fetch(pieces[half], name, half) for half, name in held],
                    now == (TURN + SLOTS - 1, STREAMS - 1),
                )
                for (half, name), array in zip(held, through):
                    pieces[half][name] = array
                senders = [s for s in range(1, SECTIONS) if 0 <= moment - TURN + s < SLOTS]
                if moment < TURN + SLOTS - 1:
                    returning[stream] = lax.ppermute(output, axes, route(senders, False))
        arriving = sent

    chips = [[replica for replica in range(REPLICAS) if replica % 2 == core] for core in range(2)]
    columns = lax.all_to_all(through[-1], "dp", 0, 0, axis_index_groups=chips)
    keep, give = product(columns, [fetch(pieces[half], name, half) for half in range(2) for name in PIECE_FROM])
    other = [(replica ^ 1, replica) for replica in range(REPLICAS)]
    blocks = add(keep, lax.ppermute(give, "dp", other))
    blocks = lax.all_to_all(blocks, "dp", 0, 0, axis_index_groups=chips)
    weight_rows, sums = finish(blocks, weights[0])
    own_gain = lax.dynamic_slice_in_dim(gains[0], lax.axis_index("dp") * SHARE, SHARE, 0)
    return (weight_rows[None], (sums[:, 0] / own_gain)[None])


def solution(mesh):
    placed = (P(None, "dp", None), P(None, "dp", None), P("chain", None, None), P("chain", None))
    return jax.shard_map(
        on_device,
        mesh=mesh,
        in_specs=placed,
        out_specs=(P("chain", "dp", None), P("chain", "dp")),
        check_vma=False,
    )
```

```python
import functools

import jax
import jax.numpy as jnp
from jax import lax
from jax.experimental import pallas as pl
from jax.experimental.pallas import tpu as pltpu
from jax.sharding import PartitionSpec as P

SECTIONS = 8
LAST = SECTIONS - 1
TURN = 2 * LAST
REPLICAS = 16
D = 3072
SPAN = 256
SHARE = D // REPLICAS
CHIPS = REPLICAS // 2
WIDE = D // CHIPS
STREAMS = 2
SLOTS = 2
ROWS = SPAN // (STREAMS * SLOTS)
COLS = 1024
PIECES = 6
PIECE = D // PIECES
TURNED = D
INPUT = 2 * D
GRAD = INPUT + SPAN
ENDS = GRAD + SPAN
HIGH = ENDS + SPAN
LOW = HIGH + SPAN
GAIN = LOW + SPAN
ARENA = GAIN + 16
HALF = SECTIONS // 2
SPLIT = HALF + SLOTS - 2
WEIGHTS = {7: 0, 8: 0, 9: 1, 10: 1, 11: 1, 13: 0, 14: 0, 15: 0}
VM = pl.BlockSpec(memory_space=pltpu.VMEM)
ANY = pl.BlockSpec(memory_space=pl.ANY)


def cost(moment):
    weight = WEIGHTS.get(moment, 20)
    return pl.CostEstimate(flops=weight * 2 * ROWS * D * D, bytes_accessed=4 * D * D, transcendentals=0)


def pin(array):
    return pltpu.with_memory_space_constraint(array, pltpu.VMEM)


def far(array):
    return pltpu.with_memory_space_constraint(array, pltpu.HBM)


def params(mib):
    return pltpu.CompilerParams(vmem_limit_bytes=mib << 20)


def partner(section, replica):
    z_hi, rest = divmod(replica, 8)
    core = rest % 2
    if section % 2 == 0 and core == 1:
        z_hi = 1 - z_hi
    return z_hi * 8 + rest


def route(sections, forward):
    pairs = []
    for section in sections:
        low = section if forward else section - 1
        for replica in range(REPLICAS):
            here, there = low * REPLICAS + replica, (low + 1) * REPLICAS + partner(low, replica)
            pairs.append((here, there) if forward else (there, here))
    return pairs


def inverse_rms(x_float):
    return lax.rsqrt(jnp.mean(x_float * x_float, axis=-1, keepdims=True) + 1e-06)


def at_slot(base, slot):
    return pl.ds(pl.multiple_of(base + slot * ROWS, ROWS), ROWS)


def gain_of(arena, part):
    three = arena[GAIN : GAIN + 16, part].astype(jnp.float32)
    return three[0:1] + three[1:2] + three[2:3]


def each_part(body):
    def run(index, carry):
        body(index, pl.ds(pl.multiple_of(index * COLS, COLS), COLS))
        return carry

    lax.fori_loop(0, D // COLS, run, 0)


def forward_block(slot, given, arena, saved, output, scaled, sem, ready=None):
    arena[at_slot(INPUT, slot)] = given
    x_float = given.astype(jnp.float32)
    scaled[...] = (x_float * inverse_rms(x_float) * gain_of(arena, slice(None))).astype(jnp.bfloat16)
    saves = [pltpu.make_async_copy(scaled, a.at[at_slot(0, slot)], sem) for a in saved]
    if len(saves) == 1:
        saves[0].start()
    else:
        low = lax.axis_index("chain") < HALF
        pl.when(low)(saves[0].start)
        pl.when(jnp.logical_not(low))(saves[1].start)

    def column_part(index, part):
        if ready is not None:
            ready(index)
        hidden = jnp.dot(scaled[...], arena[0:D, part], preferred_element_type=jnp.float32)
        high = hidden.astype(jnp.bfloat16)
        arena[at_slot(HIGH, slot), part] = high
        arena[at_slot(LOW, slot), part] = (hidden - high.astype(jnp.float32)).astype(jnp.bfloat16)
        x_part = arena[at_slot(INPUT, slot), part].astype(jnp.float32)
        output[:, part] = (x_part + jax.nn.gelu(hidden)).astype(jnp.bfloat16)

    each_part(column_part)
    saves[0].wait()


def first_kernel(weight, tokens, cotangent, gain, output, arena, saved, scaled, made, gain_row, sem, loads):
    section = lax.axis_index("chain")
    ends = arena.at[pl.ds(ENDS, SPAN)]
    load_gain = pltpu.make_async_copy(gain, gain_row, loads.at[0])
    load_tokens = pltpu.make_async_copy(tokens, ends, loads.at[1])
    load_cotangent = pltpu.make_async_copy(cotangent, ends, loads.at[1])

    def load_part(index):
        part = pl.ds(pl.multiple_of(index * COLS, COLS), COLS)
        return pltpu.make_async_copy(weight.at[:, part], arena.at[pl.ds(0, D), part], loads.at[2 + index])

    load_gain.start()

    @pl.when(section == 0)
    def _():
        load_tokens.start()

    for index in range(D // COLS):
        load_part(index).start()

    @pl.when(section == LAST)
    def _():
        load_cotangent.start()

    load_gain.wait()
    row = gain_row[...]
    high = row.astype(jnp.bfloat16).astype(jnp.float32)
    middle = (row - high).astype(jnp.bfloat16).astype(jnp.float32)
    blank = jnp.zeros((13, D), jnp.float32)
    three = jnp.concatenate([high, middle, row - high - middle, blank], axis=0)
    arena[GAIN : GAIN + 16] = three.astype(jnp.bfloat16)

    @pl.when(section == 0)
    def _():
        load_tokens.wait()
        given = arena[ENDS : ENDS + ROWS]
        forward_block(0, given, arena, [saved], made, scaled, sem, lambda index: load_part(index).wait())
        pltpu.sync_copy(made, output)

    @pl.when(section != 0)
    def _():
        for index in range(D // COLS):
            load_part(index).wait()

    @pl.when(section == LAST)
    def _():
        load_cotangent.wait()


def first(weight, tokens, cotangent, gain):
    return pl.pallas_call(
        first_kernel,
        out_shape=[
            pltpu.HBM((ROWS, D), jnp.bfloat16),
            pltpu.VMEM((ARENA, D), jnp.bfloat16),
            pltpu.HBM((SPAN, D), jnp.bfloat16),
        ],
        in_specs=[ANY] * 4,
        out_specs=[ANY, VM, ANY],
        scratch_shapes=[
            pltpu.VMEM((ROWS, D), jnp.bfloat16),
            pltpu.VMEM((ROWS, D), jnp.bfloat16),
            pltpu.VMEM((1, D), jnp.float32),
            pltpu.SemaphoreType.DMA,
            pltpu.SemaphoreType.DMA((2 + D // COLS,)),
        ],
        name="load_and_first_block",
        cost_estimate=cost(0),
        compiler_params=params(6),
    )(far(weight), far(tokens), far(cotangent), far(gain))


def turn_piece(piece, arena):
    step = 256

    def run(index, carry):
        start = pl.multiple_of(piece * PIECE + index * step, step)
        arena[TURNED : TURNED + D, pl.ds(start, step)] = arena[pl.ds(start, step), :].T
        return carry

    lax.fori_loop(0, PIECE // step, run, 0)


def forward_kernel(moment, stream, old, *refs):
    given_ref = refs[0] if moment else None
    output, arena, *saves, scaled, sem = refs[int(moment > 0) + 1 + old :]
    section = lax.axis_index("chain")
    place = moment - section
    active = jnp.logical_and(place >= 0, place < SLOTS)

    @pl.when(active)
    def _():
        start = ENDS + (stream * SLOTS + moment) * ROWS
        if moment == 0:
            given = arena[start : start + ROWS]
        elif moment < SLOTS:
            given = jnp.where(section == 0, arena[start : start + ROWS], given_ref[...])
        else:
            given = given_ref[...]
        forward_block(stream * SLOTS + place, given, arena, saves, output, scaled, sem)

    if stream == STREAMS - 1 and moment < PIECES + SLOTS:
        piece = jnp.where(place < 0, moment, moment - SLOTS)

        @pl.when(jnp.logical_and(jnp.logical_not(active), piece < PIECES))
        def _():
            turn_piece(piece, arena)


def forward(moment, stream, given, arena, saved):
    given = [given] if moment else []
    low, high = saved
    old = ([low] if moment <= SPLIT else []) + ([high] if high is not None else [])
    count = 1 + len(given)
    new = int(moment == SPLIT and high is None)
    output, arena, *kept = pl.pallas_call(
        functools.partial(forward_kernel, moment, stream, len(old)),
        out_shape=[
            pltpu.VMEM((ROWS, D), jnp.bfloat16),
            jax.ShapeDtypeStruct(arena.shape, arena.dtype),
        ]
        + [pltpu.HBM((SPAN, D), jnp.bfloat16)] * (len(old) + new),
        in_specs=[VM] * count + [ANY] * len(old),
        out_specs=[VM, VM] + [ANY] * (len(old) + new),
        input_output_aliases={count - 1 + i: 1 + i for i in range(1 + len(old))},
        scratch_shapes=[pltpu.VMEM((ROWS, D), jnp.bfloat16), pltpu.SemaphoreType.DMA],
        name=f"forward_{moment}_{stream}",
        cost_estimate=cost(moment),
        compiler_params=params(6),
    )(*given, pin(arena), *[far(a) for a in old])
    if moment <= SPLIT:
        low = kept.pop(0)
    return output, arena, (low, kept[0] if kept else None)


def backward_kernel(moment, stream, held, pack, *refs):
    given_ref = refs[0] if moment > LAST else None
    output, arena = refs[len(refs) - held - pack - 2 : len(refs) - held - pack]
    section = lax.axis_index("chain")
    place = moment - TURN + section
    slot = stream * SLOTS + place

    def upstream(part):
        start = ENDS + (stream * SLOTS + moment - LAST) * ROWS
        if moment == LAST:
            given = arena[start : start + ROWS, part]
        elif moment - LAST < SLOTS:
            given = jnp.where(section == LAST, arena[start : start + ROWS, part], given_ref[:, part])
        else:
            given = given_ref[:, part]
        return given.astype(jnp.float32)

    @pl.when(jnp.logical_and(place >= 0, place < SLOTS))
    def _():
        def gelu_part(index, total):
            part = pl.ds(pl.multiple_of(index * COLS, COLS), COLS)
            high = arena[at_slot(HIGH, slot), part].astype(jnp.float32)
            hidden = high + arena[at_slot(LOW, slot), part].astype(jnp.float32)
            _, pullback = jax.vjp(jax.nn.gelu, hidden)
            grad_hidden = pullback(upstream(part))[0].astype(jnp.bfloat16)
            arena[at_slot(GRAD, slot), part] = grad_hidden
            return total + jnp.sum(grad_hidden.astype(jnp.float32) * hidden, axis=-1, keepdims=True)

        total = lax.fori_loop(0, D // COLS, gelu_part, jnp.zeros((ROWS, 1), jnp.float32))
        if moment == TURN + SLOTS - 1:
            return

        @pl.when(section > 0)
        def _():
            inv_rms = inverse_rms(arena[at_slot(INPUT, slot)].astype(jnp.float32))
            mean = total * (1.0 / D)

            def column_part(index, part):
                grad_normed = gain_of(arena, part) * jnp.dot(
                    arena[at_slot(GRAD, slot)],
                    arena[TURNED : TURNED + D, part],
                    preferred_element_type=jnp.float32,
                )
                normed = arena[at_slot(INPUT, slot), part].astype(jnp.float32) * inv_rms
                grad_input = upstream(part) + inv_rms * (grad_normed - normed * mean)
                output[:, part] = grad_input.astype(jnp.bfloat16)

            each_part(column_part)

    if pack:
        packed = refs[-1]
        for chip in range(CHIPS):
            packed[chip] = arena[GRAD : GRAD + SPAN, chip * WIDE : (chip + 1) * WIDE].T


def backward(moment, stream, given, arena, held, pack):
    given = [given] if moment > LAST else []
    count = len(given)
    return pl.pallas_call(
        functools.partial(backward_kernel, moment, stream, len(held), int(pack)),
        out_shape=[
            jax.ShapeDtypeStruct((ROWS, D), jnp.bfloat16),
            jax.ShapeDtypeStruct(arena.shape, arena.dtype),
        ]
        + [pltpu.HBM(a.shape, a.dtype) for a in held]
        + [jax.ShapeDtypeStruct((CHIPS, WIDE, SPAN), jnp.bfloat16)] * pack,
        in_specs=[VM] * (1 + count) + [ANY] * len(held),
        out_specs=[VM, VM] + [ANY] * len(held) + [VM] * pack,
        input_output_aliases={count + i: 1 + i for i in range(1 + len(held))},
        name=f"backward_{moment}_{stream}",
        cost_estimate=cost(moment),
        compiler_params=params(6),
    )(*given, pin(arena), *[far(a) for a in held])


def product_kernel(grads, *refs):
    pieces, (keep, give, held, turned_grads, total, sems) = refs[: 2 * CHIPS], refs[2 * CHIPS :]
    replica = lax.axis_index("dp")
    z_hi, y, core = replica // 8, (replica // 2) % 4, replica % 2
    low = lax.axis_index("chain") < HALF
    chips = [(z_hi if flip == 0 else 1 - z_hi) * 4 + (y + turn) % 4 for flip, turn in PIECE_FROM]

    def load(index, half, column):
        start = pl.multiple_of(chips[index] * SPAN, SPAN)
        part = pl.ds(column * COLS, COLS)
        return pltpu.make_async_copy(
            pieces[half * CHIPS + index].at[:, part], held.at[pl.ds(start, SPAN), part], sems.at[column]
        )

    for column in range(D // COLS):
        for index in range(CHIPS):
            pl.when(low)(load(index, 0, column).start)
            pl.when(jnp.logical_not(low))(load(index, 1, column).start)
    for chip in range(CHIPS):
        turned_grads[:, chip * SPAN : (chip + 1) * SPAN] = grads[chip]
    for column in range(D // COLS):
        part = slice(column * COLS, (column + 1) * COLS)
        pltpu.make_async_copy(held.at[:, part], held.at[:, part], sems.at[column]).wait()
        total[:, part] = jnp.dot(turned_grads[...], held[:, part], preferred_element_type=jnp.float32)

    def turn(chip, carry):
        turned = total[:, pl.ds(pl.multiple_of(chip * WIDE, WIDE), WIDE)].T
        low_rows, high_rows = turned[:SHARE], turned[SHARE:]
        keep[chip] = jnp.where(core == 0, low_rows, high_rows)
        give[chip] = jnp.where(core == 0, high_rows, low_rows).astype(jnp.bfloat16)
        return carry

    lax.fori_loop(0, CHIPS, turn, 0)


def product(grads, pieces):
    block = (CHIPS, SHARE, WIDE)
    return pl.pallas_call(
        product_kernel,
        out_shape=[jax.ShapeDtypeStruct(block, jnp.float32), jax.ShapeDtypeStruct(block, jnp.bfloat16)],
        in_specs=[VM] + [ANY] * len(pieces),
        out_specs=[VM, VM],
        scratch_shapes=[
            pltpu.VMEM((CHIPS * SPAN, D), jnp.bfloat16),
            pltpu.VMEM((WIDE, CHIPS * SPAN), jnp.bfloat16),
            pltpu.VMEM((WIDE, D), jnp.float32),
            pltpu.SemaphoreType.DMA((D // COLS,)),
        ],
        name="weight_product",
        compiler_params=params(36),
    )(grads, *[far(a) for a in pieces])


def add_kernel(keep, taken, whole):
    whole[...] = (keep[...] + taken[...].astype(jnp.float32)).astype(jnp.bfloat16)


def add(keep, taken):
    return pl.pallas_call(
        add_kernel,
        out_shape=jax.ShapeDtypeStruct(taken.shape, taken.dtype),
        in_specs=[VM, VM],
        out_specs=VM,
        name="add_cores",
        compiler_params=params(24),
    )(keep, taken)


def finish_kernel(blocks, weight, rows_ref, sums_ref, own, sem):
    start = pl.multiple_of(lax.axis_index("dp") * SHARE, SHARE)
    load = pltpu.make_async_copy(weight.at[pl.ds(start, SHARE)], own, sem)
    load.start()
    for chip in range(CHIPS):
        rows_ref[:, chip * WIDE : (chip + 1) * WIDE] = blocks[chip]
    load.wait()
    total = jnp.zeros((SHARE, 1), jnp.float32)
    for chip in range(CHIPS):
        part = slice(chip * WIDE, (chip + 1) * WIDE)
        term = own[:, part].astype(jnp.float32) * blocks[chip].astype(jnp.float32)
        total = total + jnp.sum(term, axis=-1, keepdims=True)
    sums_ref[...] = total


def finish(blocks, weight):
    return pl.pallas_call(
        finish_kernel,
        out_shape=[
            jax.ShapeDtypeStruct((SHARE, D), jnp.bfloat16),
            jax.ShapeDtypeStruct((SHARE, 1), jnp.float32),
        ],
        in_specs=[VM, ANY],
        out_specs=[VM, VM],
        scratch_shapes=[pltpu.VMEM((SHARE, D), jnp.bfloat16), pltpu.SemaphoreType.DMA],
        name="weight_rows",
        compiler_params=params(12),
    )(blocks, far(weight))


PIECE_FROM = ((0, 0), (0, 3), (0, 1), (1, 0), (1, 3), (1, 1), (0, 2), (1, 2))


def along(flip, turn):
    pairs = []
    for replica in range(REPLICAS):
        z_hi, y, core = replica // 8, (replica // 2) % 4, replica % 2
        source = (z_hi ^ flip) * 8 + (y + turn) % 4 * 2 + core
        pairs.append((source, replica))
    return pairs


def bring(array, flip, turn, half):
    pairs = [
        (section * REPLICAS + source, section * REPLICAS + target)
        for section in range(half * HALF, (half + 1) * HALF)
        for source, target in along(flip, turn)
    ]
    return lax.ppermute(array, ("chain", "dp"), pairs)


FIRST = ((0, 3), (0, 1), (1, 0))
THEN = ((0, 2), (1, 3), (1, 1), (1, 2))
GATHER = ({(11, 0): FIRST + THEN}, {(12, 0): FIRST})


def fetch(pieces, name, half):
    if name not in pieces:
        flip, turn = name
        if turn == 0:
            pieces[name] = bring(fetch(pieces, (0, 0), half), 1, 0, half)
        elif turn == 2:
            way = 1 if flip else 3
            pieces[name] = bring(fetch(pieces, (flip, way), half), 0, way, half)
        else:
            pieces[name] = bring(fetch(pieces, (flip, 0), half), 0, turn, half)
    return pieces[name]


def on_device(tokens, cotangent, weights, gains):
    axes = ("chain", "dp")
    output, arena, low = first(
        weights[0], tokens.reshape(SPAN, D), cotangent.reshape(SPAN, D), gains
    )
    saved = (low, None)
    arriving = [None] * STREAMS
    returning = [None] * STREAMS
    pieces = ({}, {})
    for moment in range(TURN + SLOTS):
        sent = list(arriving)
        for stream in range(STREAMS):
            now = (moment, stream)
            if moment < LAST + SLOTS:
                if moment or stream:
                    output, arena, saved = forward(moment, stream, arriving[stream], arena, saved)
                senders = [s for s in range(LAST) if 0 <= moment // 2 * 2 + 1 - s < SLOTS + 1]
                if moment < LAST + SLOTS - 1:
                    sent[stream] = lax.ppermute(output, axes, route(senders, True))
                if now == (SPLIT, STREAMS - 1):
                    pieces[0][0, 0] = saved[0]
                if now == (LAST + SLOTS - 1, STREAMS - 1):
                    pieces[1][0, 0] = saved[1]
            if moment >= LAST:
                held = [
                    (half, name)
                    for half in range(2)
                    for name in GATHER[half].get(now, ())
                ]
                output, arena, *through = backward(
                    moment, stream, returning[stream], arena,
                    [fetch(pieces[half], name, half) for half, name in held],
                    now == (TURN + SLOTS - 1, STREAMS - 1),
                )
                for (half, name), array in zip(held, through):
                    pieces[half][name] = array
                late = LAST + (moment - LAST) // 2 * 2 + 1
                senders = [s for s in range(1, SECTIONS) if 0 <= late - TURN + s < SLOTS + 1]
                if moment < TURN + SLOTS - 1:
                    returning[stream] = lax.ppermute(output, axes, route(senders, False))
        arriving = sent

    chips = [[replica for replica in range(REPLICAS) if replica % 2 == core] for core in range(2)]
    columns = lax.all_to_all(through[-1], "dp", 0, 0, axis_index_groups=chips)
    keep, give = product(columns, [fetch(pieces[half], name, half) for half in range(2) for name in PIECE_FROM])
    other = [(replica ^ 1, replica) for replica in range(REPLICAS)]
    blocks = add(keep, lax.ppermute(give, "dp", other))
    blocks = lax.all_to_all(blocks, "dp", 0, 0, axis_index_groups=chips)
    weight_rows, sums = finish(blocks, weights[0])
    own_gain = lax.dynamic_slice_in_dim(gains[0], lax.axis_index("dp") * SHARE, SHARE, 0)
    return (weight_rows[None], (sums[:, 0] / own_gain)[None])


def solution(mesh):
    placed = (P(None, "dp", None), P(None, "dp", None), P("chain", None, None), P("chain", None))
    return jax.shard_map(
        on_device,
        mesh=mesh,
        in_specs=placed,
        out_specs=(P("chain", "dp", None), P("chain", "dp")),
        check_vma=False,
    )
```
